32 devices in a mesh: dp: 8 (over z, x), ctx: 4 (over y, core).
Axes of the slice: x: 2, y: 2, z: 4, core: 2. Of those that a mesh axis runs over, the one named last changes fastest.
Arguments:
- queries: bfloat16 [8, 4, 2, 64, 2048], P('dp', 'ctx'), may hold values from -6 to 6
- keys: bfloat16 [8, 4, 2, 64, 512], P('dp', 'ctx'), may hold values from -6 to 6
- values: bfloat16 [8, 4, 2, 64, 512], P('dp', 'ctx'), may hold values from -6 to 6
- out_grad: bfloat16 [8, 4, 2, 64, 2048], P('dp', 'ctx'), may hold values from -6 to 6
- layer_input: bfloat16 [8, 4, 2, 64, 4096], P('dp', 'ctx'), may hold values from -6 to 6
- doc_lengths: int32 [8, 16], P('dp'), may hold values from 1 to 64, as said below
Outputs:
- query_grad: bfloat16 [8, 4, 2, 64, 2048], P('dp', 'ctx')
- key_grad: bfloat16 [8, 4, 2, 64, 512], P('dp', 'ctx')
- value_grad: bfloat16 [8, 4, 2, 64, 512], P('dp', 'ctx')
- weight_grad: float32 [4096, 512], P('ctx', 'dp')
The draws below stay inside these ranges and needn't reach their ends.
Inputs may be any that keep to these rules, and one draw needn't show every extreme that they name: `doc_lengths`: each sequence is 16 documents laid end to end that fill its 512 tokens; no document is longer than 64 tokens, and one of each sequence has exactly 64.
All inputs are finite; a program needn't handle non-finite values.
Results may differ from the reference program's by a relative error of at most 0.03.
Values may be sent and summed in bfloat16 or wider, within the bound.
A program may use at most 64 MiB of HBM per device.

```python
import math
import jax
import jax.numpy as jnp
from jax import lax

HQ = 16
KVH = 4
HD = 128
D = 4096
STRETCH = 64
PAIRS = 4
SEQS = 8
SEQ = 512


def doc_layout(key):
    base_key = jax.random.fold_in(key, 17)
    offset_key, pick_key = jax.random.split(base_key)
    spans_count = 2 * PAIRS
    index_row = jnp.arange(spans_count, dtype=jnp.int32)[None, :]
    offsets = jax.random.randint(offset_key, (SEQS, spans_count), 1, STRETCH).astype(jnp.int32)
    offsets = jnp.where(index_row == spans_count - 1, jnp.minimum(offsets, STRETCH - 2), offsets)
    offsets = jnp.where(index_row == 0, 0, offsets)
    anchors = index_row * STRETCH + offsets
    ends = jnp.concatenate([anchors[:, 1:], jnp.full((SEQS, 1), SEQ, jnp.int32)], axis=1)
    spans = ends - anchors
    lowest = jnp.maximum(1, spans - STRETCH)
    highest = jnp.minimum(STRETCH, spans - 1)
    picks = jax.random.randint(pick_key, (SEQS, spans_count), 0, 1 << 20).astype(jnp.int32)
    cuts = lowest + picks % (highest - lowest + 1)
    cuts = jnp.where(index_row == 0, STRETCH, cuts)
    lengths = jnp.stack([cuts, spans - cuts], axis=2).reshape(SEQS, 2 * spans_count)
    return lengths.astype(jnp.int32)


def to_slots(natural):
    lower = natural[:, :PAIRS]
    upper = natural[:, PAIRS:][:, ::-1]
    return jnp.stack([lower, upper], axis=2)


def draw_doc_lengths(key, part):
    return doc_layout(key)


def draw_queries(key, part):
    group_size = HQ // KVH
    shape = (SEQS, SEQ, KVH, group_size, HD)
    query_key = jax.random.fold_in(key, 31)
    base = jax.random.truncated_normal(query_key, -4.0, 4.0, shape)
    natural = base.reshape(SEQS, 2 * PAIRS, STRETCH, HQ * HD)
    return to_slots(natural).astype(jnp.bfloat16)


def draw_keys(key, part):
    shape = (SEQS, SEQ, KVH, HD)
    key_key = jax.random.fold_in(key, 37)
    base = jax.random.truncated_normal(key_key, -4.0, 4.0, shape)
    natural = base.reshape(SEQS, 2 * PAIRS, STRETCH, KVH * HD)
    return to_slots(natural).astype(jnp.bfloat16)


def spiked(values, rng, source, target, parts, factor):
    owner, partner = [(jnp.arange(values.shape[dim]) // (values.shape[dim] // parts)).reshape([-1 if axis == dim else 1 for axis in range(values.ndim)]) for dim in (source, target)]
    chosen = jax.random.permutation(rng, parts)[partner]
    strong = (owner == chosen) | (owner == (partner + parts // 2) % parts)
    return jnp.where(strong, factor * values, values)


def level_of(rng, shape, cuts, low, largest):
    def one(dim, blocks):
        steps = jax.random.uniform(jax.random.fold_in(jax.random.fold_in(rng, 6), dim), (blocks,), jnp.float32, low / len(cuts), largest / len(cuts))
        return jnp.repeat(jnp.exp(steps), shape[dim] // blocks).reshape((-1,) + (1,) * (len(shape) - dim - 1))

    gain = one(*cuts[0])
    for cut in cuts[1:]:
        gain = gain * one(*cut)
    return gain


def gaussian(rng, shape, scale, bound, cuts=(), kind=jnp.bfloat16):
    result = scale * jax.random.normal(rng, shape, jnp.float32)
    if cuts:
        result = result * level_of(rng, shape, cuts, -0.22, 0.18)
    return jnp.clip(result, -bound, bound).astype(kind)


def heavy_noise(own_key, shape, width, limit, cuts, heavy, held_as=jnp.bfloat16):
    values = width * jax.random.normal(own_key, shape, jnp.float32)
    if cuts:
        values = values * level_of(own_key, shape, cuts, -0.22, 0.18)
    return jnp.clip(spiked(values, jax.random.fold_in(own_key, 3), *heavy), -limit, limit).astype(held_as)


def setup_inputs(seed: int = 0) -> dict:
    key_of = jax.random.split(jax.random.key(seed), 7)
    queries = draw_queries(jax.random.fold_in(key_of[6], 71), 0)
    keys = draw_keys(jax.random.fold_in(key_of[6], 71), 0)
    values = gaussian(key_of[2], (SEQS, PAIRS, 2, STRETCH, KVH * HD), 1.0, 6.0, ((0, 8), (1, 4)))
    out_grad = gaussian(key_of[3], (SEQS, PAIRS, 2, STRETCH, HQ * HD), 1.0, 6.0, ((0, 8), (1, 4)))
    layer_input = heavy_noise(key_of[4], (SEQS, PAIRS, 2, STRETCH, D), 1.0, 6.0, ((0, 8), (1, 4)), (1, 4, 4, 2.0))
    doc_lengths = draw_doc_lengths(jax.random.fold_in(key_of[6], 71), 0)
    return {"queries": queries, "keys": keys, "values": values, "out_grad": out_grad, "layer_input": layer_input, "doc_lengths": doc_lengths}


def doc_index(starts, positions):
    return (lax.optimization_barrier(jnp.sum((starts <= positions[..., None]).astype(jnp.int32), axis=-1)) - 1).astype(jnp.int32)

def attend(query_rows, key_block, value_block, grad_rows, query_pos, key_pos, starts):
    blocks, rows, query_width = query_rows.shape
    columns = key_block.shape[1]
    kv_heads = key_block.shape[2] // HD
    groups = query_width // HD // kv_heads
    inverse_root = 1.0 / math.sqrt(HD)
    query_heads = query_rows.reshape(blocks, rows, kv_heads, groups, HD).astype(jnp.float32)
    grad_heads = grad_rows.reshape(blocks, rows, kv_heads, groups, HD).astype(jnp.float32)
    key_heads = key_block.reshape(blocks, columns, kv_heads, HD).astype(jnp.float32)
    value_heads = value_block.reshape(blocks, columns, kv_heads, HD).astype(jnp.float32)
    query_doc = doc_index(starts, query_pos)
    key_doc = doc_index(starts, key_pos)
    allowed = (query_doc[:, :, None] == key_doc[:, None, :]) & (key_pos[:, None, :] <= query_pos[:, :, None]) & (key_pos[:, None, :] >= 0)
    scores = jnp.einsum('bqngd,bknd->bngqk', query_heads, key_heads) * inverse_root
    scores = jnp.where(allowed[:, None, None], scores, -1e+30)
    top_score = lax.optimization_barrier(jnp.max(scores, axis=-1, keepdims=True))
    log_total = top_score + jnp.log(lax.optimization_barrier(jnp.sum(jnp.exp(scores - top_score), axis=-1, keepdims=True)))
    probs = jnp.exp(scores - log_total)
    probs_low = probs.astype(jnp.bfloat16)
    attn_out = jnp.einsum('bngqk,bknd->bqngd', probs_low.astype(jnp.float32), value_heads).astype(jnp.bfloat16)
    delta = lax.optimization_barrier(jnp.sum(grad_heads * attn_out.astype(jnp.float32), axis=-1))
    dprob = jnp.einsum('bqngd,bknd->bngqk', grad_heads, value_heads)
    dscore = (probs * (dprob - jnp.transpose(delta, (0, 2, 3, 1))[..., None])).astype(jnp.bfloat16)
    dscore_wide = dscore.astype(jnp.float32)
    query_grad = (jnp.einsum('bngqk,bknd->bqngd', dscore_wide, key_heads) * inverse_root).astype(jnp.bfloat16)
    key_terms = jnp.einsum('bngqk,bqngd->bknd', dscore_wide, query_heads) * inverse_root
    value_terms = jnp.einsum('bngqk,bqngd->bknd', probs_low.astype(jnp.float32), grad_heads)
    return (query_grad.reshape(blocks, rows, query_width), key_terms.reshape(blocks, columns, kv_heads * HD), value_terms.reshape(blocks, columns, kv_heads * HD))

def natural_order(slots):
    return jnp.concatenate([slots[:, 0], slots[::-1, 1]], axis=0)

def slot_order(natural):
    return jnp.stack([natural[:PAIRS], natural[PAIRS:][::-1]], axis=1)

def one_sequence(inputs):
    query_slots, key_slots, value_slots, grad_slots, lengths = inputs
    starts = (jnp.cumsum(lengths) - lengths).astype(jnp.int32)
    query_rows = natural_order(query_slots)
    key_rows = natural_order(key_slots)
    value_rows = natural_order(value_slots)
    grad_rows = natural_order(grad_slots)
    empty_block = jnp.zeros_like(key_rows[:1])
    key_block = jnp.concatenate([jnp.concatenate([empty_block, key_rows[:-1]], axis=0), key_rows], axis=1)
    value_block = jnp.concatenate([jnp.concatenate([empty_block, value_rows[:-1]], axis=0), value_rows], axis=1)
    stretch_ids = jnp.arange(2 * PAIRS, dtype=jnp.int32)
    offsets = jnp.arange(STRETCH, dtype=jnp.int32)
    query_pos = (stretch_ids[:, None] * STRETCH + offsets[None, :]).astype(jnp.int32)
    key_pos = jnp.concatenate([query_pos - STRETCH, query_pos], axis=1).astype(jnp.int32)
    query_grad, key_terms, value_terms = attend(query_rows, key_block, value_block, grad_rows, query_pos, key_pos, starts)
    tail_zero = jnp.zeros((1, STRETCH, key_terms.shape[2]), jnp.float32)
    key_grad = key_terms[:, STRETCH:] + jnp.concatenate([key_terms[1:, :STRETCH], tail_zero], axis=0)
    value_grad = value_terms[:, STRETCH:] + jnp.concatenate([value_terms[1:, :STRETCH], tail_zero], axis=0)
    return (slot_order(query_grad), slot_order(key_grad.astype(jnp.bfloat16)), slot_order(value_grad.astype(jnp.bfloat16)))

def reference(queries, keys, values, out_grad, layer_input, doc_lengths):
    query_grad, key_grad, value_grad = lax.map(one_sequence, (queries, keys, values, out_grad, doc_lengths))
    flat_input = layer_input.reshape(SEQS * PAIRS, 2 * STRETCH, D)
    flat_values = value_grad.reshape(SEQS * PAIRS, 2 * STRETCH, KVH * HD)

    def accumulate(total, pieces):
        input_rows, value_rows = pieces
        partial_value = jnp.dot(input_rows.T, value_rows, preferred_element_type=jnp.float32).astype(jnp.bfloat16)
        partial_value = lax.optimization_barrier(partial_value)
        return (total + partial_value.astype(jnp.float32), None)
    total = lax.scan(accumulate, jnp.zeros((D, KVH * HD), jnp.float32), (flat_input, flat_values))[0]
    weight_grad = total / jnp.float32(SEQS)
    return (query_grad, key_grad, value_grad, weight_grad)
```

```python
import functools
import math

import jax
import jax.numpy as jnp
from jax import lax
from jax.experimental import pallas as pl
from jax.experimental.pallas import tpu as pltpu
from jax.sharding import PartitionSpec as P

HD = 128
MESH = pl.DeviceIdType.MESH


def dot(a, b, ca, cb):
    return lax.dot_general(a, b, (((ca,), (cb,)), ((), ())), preferred_element_type=jnp.float32)


def kernel(
    n_ctx, n_hi, n_lo, span, kvh, groups,
    q_ref, k_ref, v_ref, g_ref, li_ref, len_ref,
    dq_ref, dk_ref, dv_ref, w_ref,
    halo, sent, back, own, li_buf, vg_buf, part, recv_lo, part_hi, recv_hi, mine,
    halo_ss, halo_rs, back_ss, back_rs, li_ss, li_rs, li_own, vg_ss, vg_rs,
    lo_ss, lo_rs, hi_ss, hi_rs,
):
    me = lax.axis_index("ctx")
    place = lax.axis_index("dp")
    my_hi = place // n_lo
    my_lo = place % n_lo
    last = n_ctx - 1
    tokens = 2 * span
    chunk = li_buf.shape[1]
    blk = part.shape[2]
    inverse_root = 1.0 / math.sqrt(HD)

    def ctx_id(i):
        return (place, i)

    def dp_id(d):
        return (d, me)

    ctx_peers = [lax.rem(me + j, n_ctx) for j in range(1, n_ctx)]
    lo_peers = [lax.rem(my_lo + j, n_lo) for j in range(1, n_lo)]
    hi_peers = [lax.rem(my_hi + j, n_hi) for j in range(1, n_hi)]

    barrier = pltpu.get_barrier_semaphore()
    for peer in ctx_peers:
        pl.semaphore_signal(barrier, inc=1, device_id=ctx_id(peer), device_id_type=MESH)
    for peer in lo_peers:
        pl.semaphore_signal(barrier, inc=1, device_id=dp_id(my_hi * n_lo + peer), device_id_type=MESH)
    for peer in hi_peers:
        pl.semaphore_signal(barrier, inc=1, device_id=dp_id(peer * n_lo + my_lo), device_id_type=MESH)
    pl.semaphore_wait(barrier, n_ctx + n_lo + n_hi - 3)

    def halo_copy(slot, which):
        source = (k_ref, v_ref)[which]
        return pltpu.make_async_remote_copy(
            src_ref=source.at[pl.ds(slot * span, span)],
            dst_ref=halo.at[slot, which],
            send_sem=halo_ss.at[slot, which],
            recv_sem=halo_rs.at[slot, which],
            device_id=ctx_id(jnp.minimum(me + 1, last) if slot == 0 else jnp.maximum(me - 1, 0)),
            device_id_type=MESH,
        )

    def back_copy(slot):
        return pltpu.make_async_remote_copy(
            src_ref=sent.at[slot],
            dst_ref=back.at[slot],
            send_sem=back_ss.at[slot],
            recv_sem=back_rs.at[slot],
            device_id=ctx_id(jnp.maximum(me - 1, 0) if slot == 0 else jnp.minimum(me + 1, last)),
            device_id_type=MESH,
        )

    @pl.when(me < last)
    def _():
        for which in range(2):
            halo_copy(0, which).start()

    @pl.when(me > 0)
    def _():
        for which in range(2):
            halo_copy(1, which).start()

    def li_copy(j):
        peer = ctx_peers[j]
        return pltpu.make_async_remote_copy(
            src_ref=li_ref.at[:, pl.ds(pl.multiple_of(peer * chunk, chunk), chunk)],
            dst_ref=li_buf.at[pl.ds(pl.multiple_of(me * tokens, tokens), tokens)],
            send_sem=li_ss.at[j],
            recv_sem=li_rs.at[j],
            device_id=ctx_id(peer),
            device_id_type=MESH,
        )

    li_local = pltpu.make_async_copy(
        li_ref.at[:, pl.ds(pl.multiple_of(me * chunk, chunk), chunk)],
        li_buf.at[pl.ds(pl.multiple_of(me * tokens, tokens), tokens)],
        li_own,
    )
    li_local.start()
    for j in range(n_ctx - 1):
        li_copy(j).start()

    @pl.when(me == 0)
    def _():
        halo[0] = jnp.zeros(halo.shape[1:], halo.dtype)
        back[1] = jnp.zeros(back.shape[1:], back.dtype)

    @pl.when(me == last)
    def _():
        halo[1, 0] = k_ref[pl.ds(0, span)]
        halo[1, 1] = v_ref[pl.ds(0, span)]

    for slot in range(2):
        stretch = me if slot == 0 else 2 * n_ctx - 1 - me
        first = stretch * span
        lane = lax.broadcasted_iota(jnp.int32, (1, groups * span), 1)
        pos = first + lax.rem(lane, span)
        begin = jnp.zeros_like(pos)
        run = jnp.int32(0)
        for j in range(len_ref.shape[1]):
            begin = jnp.where(pos >= run, run, begin)
            run = run + len_ref[0, j]
        key_pos = first - span + lax.broadcasted_iota(jnp.int32, (2 * span, groups * span), 0)
        allowed = (key_pos >= begin) & (key_pos <= pos)

        @pl.when((me > 0) if slot == 0 else (me < last))
        def _():
            for which in range(2):
                halo_copy(slot, which).wait_recv()

        rows = pl.ds(slot * span, span)
        for g in range(kvh):
            col = slice(g * HD, (g + 1) * HD)
            heads = [slice(h * HD, (h + 1) * HD) for h in range(g * groups, (g + 1) * groups)]
            kk = jnp.concatenate([halo[slot, 0, :, col], k_ref[rows, col]], axis=0)
            vv = jnp.concatenate([halo[slot, 1, :, col], v_ref[rows, col]], axis=0)
            qq = jnp.concatenate([q_ref[rows, h] for h in heads], axis=0)
            gg = jnp.concatenate([g_ref[rows, h] for h in heads], axis=0)
            scores = jnp.where(allowed, dot(kk, qq, 1, 1) * inverse_root, -1e30)
            weights = jnp.exp(scores - jnp.max(scores, axis=0, keepdims=True))
            probs = weights / jnp.sum(weights, axis=0, keepdims=True)
            low = probs.astype(jnp.bfloat16)
            dprob = dot(vv, gg, 1, 1)
            delta = jnp.sum(low.astype(jnp.float32) * dprob, axis=0, keepdims=True)
            ds = (probs * (dprob - delta)).astype(jnp.bfloat16)
            dk = dot(ds, qq, 1, 0) * inverse_root
            dv = dot(low, gg, 1, 0)
            dq = (dot(ds, kk, 0, 0) * inverse_root).astype(jnp.bfloat16)
            for n, h in enumerate(heads):
                dq_ref[rows, h] = dq[n * span : (n + 1) * span]
            sent[slot, 0, :, col] = dk[:span].astype(jnp.bfloat16)
            sent[slot, 1, :, col] = dv[:span].astype(jnp.bfloat16)
            own[slot, 0, :, col] = dk[span:]
            own[slot, 1, :, col] = dv[span:]

        @pl.when((me > 0) if slot == 0 else (me < last))
        def _():
            back_copy(slot).start()

    @pl.when(me == last)
    def _():
        back[0] = sent[1]

    my_rows = pl.ds(pl.multiple_of(me * tokens, tokens), tokens)
    for slot in range(2):
        @pl.when((me < last) if slot == 0 else (me > 0))
        def _():
            back_copy(slot).wait_recv()

        rows = pl.ds(slot * span, span)
        dv_ref[rows] = (own[slot, 1] + back[slot, 1].astype(jnp.float32)).astype(jnp.bfloat16)

    def vg_copy(j):
        return pltpu.make_async_remote_copy(
            src_ref=dv_ref,
            dst_ref=vg_buf.at[my_rows],
            send_sem=vg_ss.at[j],
            recv_sem=vg_rs.at[j],
            device_id=ctx_id(ctx_peers[j]),
            device_id_type=MESH,
        )

    for j in range(n_ctx - 1):
        vg_copy(j).start()
    vg_buf[my_rows] = dv_ref[...]
    for slot in range(2):
        rows = pl.ds(slot * span, span)
        dk_ref[rows] = (own[slot, 0] + back[slot, 0].astype(jnp.float32)).astype(jnp.bfloat16)
    li_local.wait()
    for j in range(n_ctx - 1):
        li_copy(j).wait_recv()
    for j in range(n_ctx - 1):
        vg_copy(j).wait_recv()

    def lo_copy(h, j):
        peer = lo_peers[j]
        return pltpu.make_async_remote_copy(
            src_ref=part.at[peer, h],
            dst_ref=recv_lo.at[j, h],
            send_sem=lo_ss.at[j, h],
            recv_sem=lo_rs.at[j, h],
            device_id=dp_id(my_hi * n_lo + peer),
            device_id_type=MESH,
        )

    wide = n_lo * blk
    for h in range(n_hi):
        product = dot(vg_buf[:, h * wide : (h + 1) * wide], li_buf[...], 0, 0)
        for l in range(n_lo):
            part[l, h] = product[l * blk : (l + 1) * blk].astype(jnp.bfloat16)
        for j in range(n_lo - 1):
            lo_copy(h, j).start()

    def hi_send(h):
        return pltpu.make_async_remote_copy(
            src_ref=part_hi.at[h],
            dst_ref=recv_hi.at[lax.rem(my_hi - h + n_hi, n_hi)],
            send_sem=hi_ss.at[h],
            recv_sem=hi_rs.at[lax.rem(my_hi - h + n_hi, n_hi)],
            device_id=dp_id(h * n_lo + my_lo),
            device_id_type=MESH,
        )

    for h in range(n_hi):
        for j in range(n_lo - 1):
            lo_copy(h, j).wait_recv()
        total = part[my_lo, h].astype(jnp.float32)
        for j in range(n_lo - 1):
            total = total + recv_lo[j, h].astype(jnp.float32)

        @pl.when(my_hi == h)
        def _():
            mine[...] = total

        @pl.when(my_hi != h)
        def _():
            part_hi[h] = total.astype(jnp.bfloat16)
            hi_send(h).start()

    def hi_recv(d):
        return pltpu.make_async_remote_copy(
            src_ref=part_hi.at[0],
            dst_ref=recv_hi.at[d],
            send_sem=hi_ss.at[0],
            recv_sem=hi_rs.at[d],
            device_id=dp_id(hi_peers[d - 1] * n_lo + my_lo),
            device_id_type=MESH,
        )

    for d in range(1, n_hi):
        hi_recv(d).wait_recv()
    total = mine[...]
    for d in range(1, n_hi):
        total = total + recv_hi[d].astype(jnp.float32)
    w_ref[...] = total * (1.0 / (n_hi * n_lo))

    @pl.when(me < last)
    def _():
        for which in range(2):
            halo_copy(0, which).wait_send()
        back_copy(1).wait_send()

    @pl.when(me > 0)
    def _():
        for which in range(2):
            halo_copy(1, which).wait_send()
        back_copy(0).wait_send()

    for j in range(n_ctx - 1):
        li_copy(j).wait_send()
        vg_copy(j).wait_send()
    for h in range(n_hi):
        for j in range(n_lo - 1):
            lo_copy(h, j).wait_send()

        @pl.when(my_hi != h)
        def _():
            hi_send(h).wait_send()


def body(n_ctx, n_dp, queries, keys, values, out_grad, layer_input, doc_lengths):
    span = queries.shape[3]
    tokens = 2 * span
    q = queries.reshape(tokens, queries.shape[4])
    k = keys.reshape(tokens, keys.shape[4])
    v = values.reshape(tokens, values.shape[4])
    g = out_grad.reshape(tokens, out_grad.shape[4])
    li = layer_input.reshape(tokens, layer_input.shape[4])
    kv_width = k.shape[1]
    kvh = kv_width // HD
    groups = q.shape[1] // kv_width
    chunk = li.shape[1] // n_ctx
    blk = kv_width // n_dp
    n_lo = 2 ** ((n_dp.bit_length() - 1) // 2)
    n_hi = n_dp // n_lo
    bf16, f32 = jnp.bfloat16, jnp.float32
    dma = pltpu.SemaphoreType.DMA
    vmem = pl.BlockSpec(memory_space=pltpu.VMEM)
    outs = pl.pallas_call(
        functools.partial(kernel, n_ctx, n_hi, n_lo, span, kvh, groups),
        out_shape=(
            jax.ShapeDtypeStruct(q.shape, bf16),
            jax.ShapeDtypeStruct(k.shape, bf16),
            jax.ShapeDtypeStruct(v.shape, bf16),
            jax.ShapeDtypeStruct((blk, chunk), f32),
        ),
        in_specs=[vmem, vmem, vmem, vmem, pl.BlockSpec(memory_space=pl.ANY),
                  pl.BlockSpec(memory_space=pltpu.SMEM)],
        out_specs=(vmem, vmem, vmem, vmem),
        scratch_shapes=[
            pltpu.VMEM((2, 2, span, kv_width), bf16),
            pltpu.VMEM((2, 2, span, kv_width), bf16),
            pltpu.VMEM((2, 2, span, kv_width), bf16),
            pltpu.VMEM((2, 2, span, kv_width), f32),
            pltpu.VMEM((n_ctx * tokens, chunk), bf16),
            pltpu.VMEM((n_ctx * tokens, kv_width), bf16),
            pltpu.VMEM((n_lo, n_hi, blk, chunk), bf16),
            pltpu.VMEM((n_lo - 1, n_hi, blk, chunk), bf16),
            pltpu.VMEM((n_hi, blk, chunk), bf16),
            pltpu.VMEM((n_hi, blk, chunk), bf16),
            pltpu.VMEM((blk, chunk), f32),
            dma((2, 2)), dma((2, 2)), dma((2,)), dma((2,)),
            dma((n_ctx - 1,)), dma((n_ctx - 1,)), dma,
            dma((n_ctx - 1,)), dma((n_ctx - 1,)),
            dma((n_lo - 1, n_hi)), dma((n_lo - 1, n_hi)), dma((n_hi,)), dma((n_hi,)),
        ],
        compiler_params=pltpu.CompilerParams(
            collective_id=0, has_side_effects=True, vmem_limit_bytes=40 * 1024 * 1024
        ),
        name="attention_grads",
    )(q, k, v, g, li, doc_lengths)
    dq, dk, dv, w = outs
    return (
        dq.reshape(queries.shape),
        dk.reshape(keys.shape),
        dv.reshape(values.shape),
        w.T,
    )


def solution(mesh):
    tokens = P("dp", "ctx", None, None, None)
    return jax.shard_map(
        functools.partial(body, mesh.shape["ctx"], mesh.shape["dp"]),
        mesh=mesh,
        in_specs=(tokens, tokens, tokens, tokens, tokens, P("dp", None)),
        out_specs=(tokens, tokens, tokens, P("ctx", "dp")),
        check_vma=False,
    )
```

```python
import functools
import math

import jax
import jax.numpy as jnp
from jax import lax
from jax.experimental import pallas as pl
from jax.experimental.pallas import tpu as pltpu
from jax.sharding import PartitionSpec as P

HD = 128
MESH = pl.DeviceIdType.MESH
VMEM_LIMIT = 63 * 1024 * 1024


def dot(a, b, ca, cb):
    return lax.dot_general(a, b, (((ca,), (cb,)), ((), ())), preferred_element_type=jnp.float32)


def kernel(
    n_ctx, n_hi, n_lo, span, kvh, groups,
    q_hbm, k_hbm, v_hbm, g_hbm, li_ref, len_hbm,
    dq_hbm, dk_hbm, dv_hbm, w_hbm,
    dq_ref, dk_ref, dv_ref, w_ref, out_sem,
    q_ref, g_ref, len_ref, kv, sent, back, own, li_buf, vg_buf, part, recv_lo, part_hi, recv_hi,
    in_sem, kv_sem, fold_sem, halo_ss, halo_rs, back_ss, back_rs, li_ss, li_rs, li_own,
    pair_ss, pair_rs, vg_ss, vg_rs, fwd_ss, fwd_rs, lo_ss, lo_rs, hi_ss, hi_rs,
):
    me = lax.axis_index("ctx")
    place = lax.axis_index("dp")
    my_hi = place // n_lo
    my_lo = place % n_lo
    last = n_ctx - 1
    tokens = 2 * span
    chunk = li_buf.shape[1]
    pieces, _, blk, width = part.shape[1:]
    inverse_root = 1.0 / math.sqrt(HD)

    def ctx_id(i):
        return (place, i)

    def dp_id(d):
        return (d, me)

    partner = me + 1 - 2 * lax.rem(me, 2)
    same_core = [lax.rem(me + 2 * j, n_ctx) for j in range(1, n_ctx // 2)]
    ctx_peers = [lax.rem(me + j, n_ctx) for j in range(1, n_ctx)]
    lo_peers = [lax.rem(my_lo + j, n_lo) for j in range(1, n_lo)]
    hi_peers = [lax.rem(my_hi + j, n_hi) for j in range(1, n_hi)]

    locals_in = [
        pltpu.make_async_copy(len_hbm, len_ref, in_sem.at[0]),
        pltpu.make_async_copy(q_hbm, q_ref, in_sem.at[1]),
        pltpu.make_async_copy(g_hbm, g_ref, in_sem.at[2]),
    ]
    own_kv = [
        pltpu.make_async_copy(
            source.at[pl.ds(slot * span, span)],
            kv.at[slot, which, pl.ds(span, span)],
            kv_sem.at[slot, which],
        )
        for slot in range(2)
        for which, source in enumerate((k_hbm, v_hbm))
    ]
    fold_kv = [
        pltpu.make_async_copy(
            source.at[pl.ds(0, span)], kv.at[1, which, pl.ds(0, span)], fold_sem.at[which]
        )
        for which, source in enumerate((k_hbm, v_hbm))
    ]
    my_rows = pl.ds(pl.multiple_of(me * tokens, tokens), tokens)
    li_local = pltpu.make_async_copy(
        li_ref.at[:, pl.ds(pl.multiple_of(me * chunk, chunk), chunk)], li_buf.at[my_rows], li_own
    )
    for copy in own_kv + locals_in:
        copy.start()

    barrier = pltpu.get_barrier_semaphore()
    for peer in ctx_peers:
        pl.semaphore_signal(barrier, inc=1, device_id=ctx_id(peer), device_id_type=MESH)
    for peer in lo_peers:
        pl.semaphore_signal(barrier, inc=1, device_id=dp_id(my_hi * n_lo + peer), device_id_type=MESH)
    for peer in hi_peers:
        pl.semaphore_signal(barrier, inc=1, device_id=dp_id(peer * n_lo + my_lo), device_id_type=MESH)

    @pl.when(me == 0)
    def _():
        kv[0, :, pl.ds(0, span)] = jnp.zeros((2, span, kv.shape[3]), kv.dtype)
        back[1] = jnp.zeros(back.shape[1:], back.dtype)

    @pl.when(me == last)
    def _():
        for copy in fold_kv:
            copy.start()

    pl.semaphore_wait(barrier, n_ctx + n_lo + n_hi - 3)

    def halo_copy(slot, which):
        source = (k_hbm, v_hbm)[which]
        return pltpu.make_async_remote_copy(
            src_ref=source.at[pl.ds(slot * span, span)],
            dst_ref=kv.at[slot, which, pl.ds(0, span)],
            send_sem=halo_ss.at[slot, which],
            recv_sem=halo_rs.at[slot, which],
            device_id=ctx_id(jnp.minimum(me + 1, last) if slot == 0 else jnp.maximum(me - 1, 0)),
            device_id_type=MESH,
        )

    def back_copy(slot):
        return pltpu.make_async_remote_copy(
            src_ref=sent.at[slot],
            dst_ref=back.at[slot],
            send_sem=back_ss.at[slot],
            recv_sem=back_rs.at[slot],
            device_id=ctx_id(jnp.maximum(me - 1, 0) if slot == 0 else jnp.minimum(me + 1, last)),
            device_id_type=MESH,
        )

    @pl.when(me < last)
    def _():
        for which in range(2):
            halo_copy(0, which).start()

    @pl.when(me > 0)
    def _():
        for which in range(2):
            halo_copy(1, which).start()

    def li_copy(j):
        peer = ctx_peers[j]
        return pltpu.make_async_remote_copy(
            src_ref=li_ref.at[:, pl.ds(pl.multiple_of(peer * chunk, chunk), chunk)],
            dst_ref=li_buf.at[my_rows],
            send_sem=li_ss.at[j],
            recv_sem=li_rs.at[j],
            device_id=ctx_id(peer),
            device_id_type=MESH,
        )

    for j in range(n_ctx - 1):
        li_copy(j).start()
    li_local.start()
    for copy in own_kv + locals_in:
        copy.wait()

    for slot in range(2):
        stretch = me if slot == 0 else 2 * n_ctx - 1 - me
        first = stretch * span
        lane = lax.broadcasted_iota(jnp.int32, (1, groups * span), 1)
        pos = first + lax.rem(lane, span)
        begin = jnp.zeros_like(pos)
        run = jnp.int32(0)
        for j in range(len_ref.shape[1]):
            begin = jnp.where(pos >= run, run, begin)
            run = run + len_ref[0, j]
        key_pos = first - span + lax.broadcasted_iota(jnp.int32, (2 * span, groups * span), 0)
        allowed = (key_pos >= begin) & (key_pos <= pos)

        @pl.when((me > 0) if slot == 0 else (me < last))
        def _():
            for which in range(2):
                halo_copy(slot, which).wait_recv()

        if slot == 1:
            @pl.when(me == last)
            def _():
                for copy in fold_kv:
                    copy.wait()

        rows = pl.ds(slot * span, span)
        for g in range(kvh):
            col = slice(g * HD, (g + 1) * HD)
            heads = [slice(h * HD, (h + 1) * HD) for h in range(g * groups, (g + 1) * groups)]
            kk = kv[slot, 0, :, col]
            vv = kv[slot, 1, :, col]
            qq = jnp.concatenate([q_ref[rows, h] for h in heads], axis=0)
            gg = jnp.concatenate([g_ref[rows, h] for h in heads], axis=0)
            scores = jnp.where(allowed, dot(kk, qq, 1, 1) * inverse_root, -1e30)
            weights = jnp.exp(scores - jnp.max(scores, axis=0, keepdims=True))
            probs = weights * (1.0 / jnp.sum(weights, axis=0, keepdims=True))
            low = probs.astype(jnp.bfloat16)
            dprob = dot(vv, gg, 1, 1)
            delta = jnp.sum(low.astype(jnp.float32) * dprob, axis=0, keepdims=True)
            ds = (probs * (dprob - delta)).astype(jnp.bfloat16)
            dk = dot(ds, qq, 1, 0) * inverse_root
            dv = dot(low, gg, 1, 0)
            dq = (dot(ds, kk, 0, 0) * inverse_root).astype(jnp.bfloat16)
            for n, h in enumerate(heads):
                dq_ref[rows, h] = dq[n * span : (n + 1) * span]
            sent[slot, 0, :, col] = dk[:span].astype(jnp.bfloat16)
            sent[slot, 1, :, col] = dv[:span].astype(jnp.bfloat16)
            own[slot, 0, :, col] = dk[span:]
            own[slot, 1, :, col] = dv[span:]

        @pl.when((me > 0) if slot == 0 else (me < last))
        def _():
            back_copy(slot).start()

    outs = [
        pltpu.make_async_copy(dq_ref, dq_hbm, out_sem.at[0]),
        pltpu.make_async_copy(dv_ref, dv_hbm, out_sem.at[1]),
        pltpu.make_async_copy(dk_ref, dk_hbm, out_sem.at[2]),
        pltpu.make_async_copy(w_ref, w_hbm, out_sem.at[3]),
    ]
    outs[0].start()

    @pl.when(me == last)
    def _():
        back[0] = sent[1]

    for slot in range(2):
        @pl.when((me < last) if slot == 0 else (me > 0))
        def _():
            back_copy(slot).wait_recv()

        rows = pl.ds(slot * span, span)
        dv_ref[rows] = (own[slot, 1] + back[slot, 1].astype(jnp.float32)).astype(jnp.bfloat16)

    def columns(i):
        return pl.ds(pl.multiple_of(i * tokens, tokens), tokens)

    def vg_send(source, target, send_sem, recv_sem):
        return pltpu.make_async_remote_copy(
            src_ref=vg_buf.at[:, columns(source)],
            dst_ref=vg_buf.at[:, columns(source)],
            send_sem=send_sem,
            recv_sem=recv_sem,
            device_id=ctx_id(target),
            device_id_type=MESH,
        )

    vg_buf[:, columns(me)] = dv_ref[...].T
    far = range(n_ctx // 2 - 1)
    for j in far:
        vg_send(me, same_core[j], vg_ss.at[j], vg_rs.at[j]).start()
    pair = vg_send(me, partner, pair_ss, pair_rs)
    pair.start()
    for slot in range(2):
        rows = pl.ds(slot * span, span)
        dk_ref[rows] = (own[slot, 0] + back[slot, 0].astype(jnp.float32)).astype(jnp.bfloat16)
    outs[1].start()
    outs[2].start()
    li_local.wait()
    for j in range(n_ctx - 1):
        li_copy(j).wait_recv()

    def forward(j):
        source = lax.rem(me - 2 * (j + 1) + n_ctx, n_ctx)
        return vg_send(source, partner, fwd_ss.at[j], fwd_rs.at[j])

    for j in far:
        vg_send(me, same_core[j], vg_ss.at[j], vg_rs.at[j]).wait_recv()
        forward(j).start()
    pair.wait_recv()
    for j in far:
        forward(j).wait_recv()

    def lo_copy(c, j):
        peer = lo_peers[j]
        return pltpu.make_async_remote_copy(
            src_ref=part.at[peer, c],
            dst_ref=recv_lo.at[j, c],
            send_sem=lo_ss.at[j, c],
            recv_sem=lo_rs.at[j, c],
            device_id=dp_id(my_hi * n_lo + peer),
            device_id_type=MESH,
        )

    for c in range(pieces):
        product = dot(vg_buf[...], li_buf[:, c * width : (c + 1) * width], 1, 0)
        for h in range(n_hi):
            for l in range(n_lo):
                top = (h * n_lo + l) * blk
                part[l, c, h] = product[top : top + blk].astype(jnp.bfloat16)
        for j in range(n_lo - 1):
            lo_copy(c, j).start()

    def hi_copy(c, j):
        return pltpu.make_async_remote_copy(
            src_ref=part_hi.at[c, hi_peers[j]],
            dst_ref=recv_hi.at[c, j],
            send_sem=hi_ss.at[c, j],
            recv_sem=hi_rs.at[c, j],
            device_id=dp_id(hi_peers[j] * n_lo + my_lo),
            device_id_type=MESH,
        )

    for c in range(pieces):
        for j in range(n_lo - 1):
            lo_copy(c, j).wait_recv()
        total = part[my_lo, c].astype(jnp.float32)
        for j in range(n_lo - 1):
            total = total + recv_lo[j, c].astype(jnp.float32)
        part_hi[c] = total.astype(jnp.bfloat16)
        for j in range(n_hi - 1):
            hi_copy(c, j).start()

    for c in range(pieces):
        total = part[my_lo, c, my_hi].astype(jnp.float32)
        for j in range(n_lo - 1):
            total = total + recv_lo[j, c, my_hi].astype(jnp.float32)
        for j in range(n_hi - 1):
            hi_copy(c, j).wait_recv()
            total = total + recv_hi[c, j].astype(jnp.float32)
        w_ref[:, c * width : (c + 1) * width] = total * (1.0 / (n_hi * n_lo))
    outs[3].start()

    @pl.when(me < last)
    def _():
        for which in range(2):
            halo_copy(0, which).wait_send()
        back_copy(1).wait_send()

    @pl.when(me > 0)
    def _():
        for which in range(2):
            halo_copy(1, which).wait_send()
        back_copy(0).wait_send()

    for j in range(n_ctx - 1):
        li_copy(j).wait_send()
    pair.wait_send()
    for j in far:
        vg_send(me, same_core[j], vg_ss.at[j], vg_rs.at[j]).wait_send()
        forward(j).wait_send()
    for c in range(pieces):
        for j in range(n_lo - 1):
            lo_copy(c, j).wait_send()
        for j in range(n_hi - 1):
            hi_copy(c, j).wait_send()
    for copy in outs:
        copy.wait()


def hand_over(*refs):
    count = len(refs) // 2
    copies = [
        pltpu.make_async_copy(refs[n], refs[count + n], refs[-1].at[n]) for n in range(count)
    ]
    for copy in copies:
        copy.start()
    for copy in copies:
        copy.wait()


def body(n_ctx, n_dp, queries, keys, values, out_grad, layer_input, doc_lengths):
    span = queries.shape[3]
    tokens = 2 * span
    q = queries.reshape(tokens, queries.shape[4])
    k = keys.reshape(tokens, keys.shape[4])
    v = values.reshape(tokens, values.shape[4])
    g = out_grad.reshape(tokens, out_grad.shape[4])
    li = layer_input.reshape(tokens, layer_input.shape[4])
    kv_width = k.shape[1]
    kvh = kv_width // HD
    groups = q.shape[1] // kv_width
    chunk = li.shape[1] // n_ctx
    blk = kv_width // n_dp
    n_lo = 2 ** ((n_dp.bit_length() - 1) // 2)
    n_hi = n_dp // n_lo
    width = min(256, chunk)
    pieces = chunk // width
    far = max(1, n_ctx // 2 - 1)
    bf16, f32 = jnp.bfloat16, jnp.float32
    dma = pltpu.SemaphoreType.DMA
    hbm = pl.BlockSpec(memory_space=pltpu.HBM)
    shapes = (
        jax.ShapeDtypeStruct(q.shape, bf16),
        jax.ShapeDtypeStruct(k.shape, bf16),
        jax.ShapeDtypeStruct(v.shape, bf16),
        jax.ShapeDtypeStruct((blk, chunk), f32),
    )
    outs = pl.pallas_call(
        functools.partial(kernel, n_ctx, n_hi, n_lo, span, kvh, groups),
        out_shape=shapes,
        in_specs=[hbm] * 6,
        out_specs=(hbm,) * 4,
        scratch_shapes=[
            pltpu.VMEM(q.shape, bf16),
            pltpu.VMEM(k.shape, bf16),
            pltpu.VMEM(v.shape, bf16),
            pltpu.VMEM((blk, chunk), f32),
            dma((4,)),
            pltpu.VMEM(q.shape, bf16),
            pltpu.VMEM(g.shape, bf16),
            pltpu.SMEM(doc_lengths.shape, jnp.int32),
            pltpu.VMEM((2, 2, 2 * span, kv_width), bf16),
            pltpu.VMEM((2, 2, span, kv_width), bf16),
            pltpu.VMEM((2, 2, span, kv_width), bf16),
            pltpu.VMEM((2, 2, span, kv_width), f32),
            pltpu.VMEM((n_ctx * tokens, chunk), bf16),
            pltpu.VMEM((kv_width, n_ctx * tokens), bf16),
            pltpu.VMEM((n_lo, pieces, n_hi, blk, width), bf16),
            pltpu.VMEM((n_lo - 1, pieces, n_hi, blk, width), bf16),
            pltpu.VMEM((pieces, n_hi, blk, width), bf16),
            pltpu.VMEM((pieces, n_hi - 1, blk, width), bf16),
            dma((3,)), dma((2, 2)), dma((2,)),
            dma((2, 2)), dma((2, 2)), dma((2,)), dma((2,)),
            dma((n_ctx - 1,)), dma((n_ctx - 1,)), dma,
            dma, dma, dma((far,)), dma((far,)), dma((far,)), dma((far,)),
            dma((n_lo - 1, pieces)), dma((n_lo - 1, pieces)),
            dma((pieces, n_hi - 1)), dma((pieces, n_hi - 1)),
        ],
        compiler_params=pltpu.CompilerParams(
            collective_id=0, has_side_effects=True, vmem_limit_bytes=VMEM_LIMIT
        ),
        name="attention_grads",
    )(q, k, v, g, li, doc_lengths)
    dq, dk, dv, w = pl.pallas_call(
        hand_over,
        out_shape=shapes,
        in_specs=[hbm] * 4,
        out_specs=(hbm,) * 4,
        scratch_shapes=[dma((4,))],
        compiler_params=pltpu.CompilerParams(vmem_limit_bytes=VMEM_LIMIT),
        name="hand_over",
    )(*outs)
    return (
        dq.reshape(queries.shape),
        dk.reshape(keys.shape),
        dv.reshape(values.shape),
        w.T,
    )


def solution(mesh):
    tokens = P("dp", "ctx", None, None, None)
    return jax.shard_map(
        functools.partial(body, mesh.shape["ctx"], mesh.shape["dp"]),
        mesh=mesh,
        in_specs=(tokens, tokens, tokens, tokens, tokens, P("dp", None)),
        out_specs=(tokens, tokens, tokens, P("ctx", "dp")),
        check_vma=False,
    )
```

```python
import functools
import math

import jax
import jax.numpy as jnp
from jax import lax
from jax.experimental import pallas as pl
from jax.experimental.pallas import tpu as pltpu
from jax.sharding import PartitionSpec as P

HD = 128
MESH = pl.DeviceIdType.MESH
VMEM_LIMIT = 63 * 1024 * 1024


def dot(a, b, ca, cb):
    return lax.dot_general(a, b, (((ca,), (cb,)), ((), ())), preferred_element_type=jnp.float32)


def kernel(
    n_ctx, n_hi, n_lo, span, kvh, groups,
    q_hbm, k_hbm, v_hbm, g_hbm, li_ref, len_hbm,
    dq_hbm, dk_hbm, dv_hbm, w_hbm,
    dq_ref, dk_ref, dv_ref, w_ref, out_sem,
    q_ref, g_ref, len_ref, kv, sent, back, own, li_buf, vg_buf, part, recv_lo, part_hi, recv_hi,
    in_sem, kv_sem, fold_sem, halo_ss, halo_rs, back_ss, back_rs, li_ss, li_rs, li_own,
    pair_ss, pair_rs, vg_ss, vg_rs, fwd_ss, fwd_rs, lo_ss, lo_rs, hi_ss, hi_rs,
):
    me = lax.axis_index("ctx")
    place = lax.axis_index("dp")
    my_hi = place // n_lo
    my_lo = place % n_lo
    last = n_ctx - 1
    tokens = 2 * span
    chunk = li_buf.shape[1]
    pieces, _, blk, width = part.shape[1:]
    inverse_root = 1.0 / math.sqrt(HD)

    def ctx_id(i):
        return (place, i)

    def dp_id(d):
        return (d, me)

    partner = me + 1 - 2 * lax.rem(me, 2)
    same_core = [lax.rem(me + 2 * j, n_ctx) for j in range(1, n_ctx // 2)]
    ctx_peers = [lax.rem(me + j, n_ctx) for j in range(1, n_ctx)]
    lo_peers = [lax.rem(my_lo + j, n_lo) for j in range(1, n_lo)]
    hi_peers = [lax.rem(my_hi + j, n_hi) for j in range(1, n_hi)]

    locals_in = [
        pltpu.make_async_copy(len_hbm, len_ref, in_sem.at[0]),
        pltpu.make_async_copy(q_hbm, q_ref, in_sem.at[1]),
        pltpu.make_async_copy(g_hbm, g_ref, in_sem.at[2]),
    ]
    own_kv = [
        pltpu.make_async_copy(
            source.at[pl.ds(slot * span, span)],
            kv.at[slot, which, pl.ds(span, span)],
            kv_sem.at[slot, which],
        )
        for slot in range(2)
        for which, source in enumerate((k_hbm, v_hbm))
    ]
    fold_kv = [
        pltpu.make_async_copy(
            source.at[pl.ds(0, span)], kv.at[1, which, pl.ds(0, span)], fold_sem.at[which]
        )
        for which, source in enumerate((k_hbm, v_hbm))
    ]
    my_rows = pl.ds(pl.multiple_of(me * tokens, tokens), tokens)
    li_local = pltpu.make_async_copy(
        li_ref.at[:, pl.ds(pl.multiple_of(me * chunk, chunk), chunk)], li_buf.at[my_rows], li_own
    )
    for copy in own_kv + locals_in:
        copy.start()

    barrier = pltpu.get_barrier_semaphore()
    for peer in ctx_peers:
        pl.semaphore_signal(barrier, inc=1, device_id=ctx_id(peer), device_id_type=MESH)
    for peer in lo_peers:
        pl.semaphore_signal(barrier, inc=1, device_id=dp_id(my_hi * n_lo + peer), device_id_type=MESH)
    for peer in hi_peers:
        pl.semaphore_signal(barrier, inc=1, device_id=dp_id(peer * n_lo + my_lo), device_id_type=MESH)

    @pl.when(me == 0)
    def _():
        kv[0, :, pl.ds(0, span)] = jnp.zeros((2, span, kv.shape[3]), kv.dtype)
        back[1] = jnp.zeros(back.shape[1:], back.dtype)

    @pl.when(me == last)
    def _():
        for copy in fold_kv:
            copy.start()

    pl.semaphore_wait(barrier, n_ctx + n_lo + n_hi - 3)

    def halo_copy(slot, which):
        source = (k_hbm, v_hbm)[which]
        return pltpu.make_async_remote_copy(
            src_ref=source.at[pl.ds(slot * span, span)],
            dst_ref=kv.at[slot, which, pl.ds(0, span)],
            send_sem=halo_ss.at[slot, which],
            recv_sem=halo_rs.at[slot, which],
            device_id=ctx_id(jnp.minimum(me + 1, last) if slot == 0 else jnp.maximum(me - 1, 0)),
            device_id_type=MESH,
        )

    def back_copy(slot):
        return pltpu.make_async_remote_copy(
            src_ref=sent.at[slot],
            dst_ref=back.at[slot],
            send_sem=back_ss.at[slot],
            recv_sem=back_rs.at[slot],
            device_id=ctx_id(jnp.maximum(me - 1, 0) if slot == 0 else jnp.minimum(me + 1, last)),
            device_id_type=MESH,
        )

    @pl.when(me < last)
    def _():
        for which in range(2):
            halo_copy(0, which).start()

    @pl.when(me > 0)
    def _():
        for which in range(2):
            halo_copy(1, which).start()

    def li_copy(j):
        peer = ctx_peers[j]
        return pltpu.make_async_remote_copy(
            src_ref=li_ref.at[:, pl.ds(pl.multiple_of(peer * chunk, chunk), chunk)],
            dst_ref=li_buf.at[my_rows],
            send_sem=li_ss.at[j],
            recv_sem=li_rs.at[j],
            device_id=ctx_id(peer),
            device_id_type=MESH,
        )

    for j in range(n_ctx - 1):
        li_copy(j).start()
    li_local.start()
    for copy in own_kv + locals_in:
        copy.wait()

    for slot in range(2):
        stretch = me if slot == 0 else 2 * n_ctx - 1 - me
        first = stretch * span
        lane = lax.broadcasted_iota(jnp.int32, (1, groups * span), 1)
        pos = first + lax.rem(lane, span)
        begin = jnp.zeros_like(pos)
        run = jnp.int32(0)
        for j in range(len_ref.shape[1]):
            begin = jnp.where(pos >= run, run, begin)
            run = run + len_ref[0, j]
        key_pos = first - span + lax.broadcasted_iota(jnp.int32, (2 * span, groups * span), 0)
        allowed = (key_pos >= begin) & (key_pos <= pos)

        @pl.when((me > 0) if slot == 0 else (me < last))
        def _():
            for which in range(2):
                halo_copy(slot, which).wait_recv()

        if slot == 1:
            @pl.when(me == last)
            def _():
                for copy in fold_kv:
                    copy.wait()

        rows = pl.ds(slot * span, span)
        for g in range(kvh):
            col = slice(g * HD, (g + 1) * HD)
            heads = [slice(h * HD, (h + 1) * HD) for h in range(g * groups, (g + 1) * groups)]
            kk = kv[slot, 0, :, col]
            vv = kv[slot, 1, :, col]
            qq = jnp.concatenate([q_ref[rows, h] for h in heads], axis=0)
            gg = jnp.concatenate([g_ref[rows, h] for h in heads], axis=0)
            scores = jnp.where(allowed, dot(kk, qq, 1, 1) * inverse_root, -1e30)
            weights = jnp.exp(scores - jnp.max(scores, axis=0, keepdims=True))
            probs = weights * (1.0 / jnp.sum(weights, axis=0, keepdims=True))
            low = probs.astype(jnp.bfloat16)
            dprob = dot(vv, gg, 1, 1)
            delta = jnp.sum(low.astype(jnp.float32) * dprob, axis=0, keepdims=True)
            ds = (probs * (dprob - delta)).astype(jnp.bfloat16)
            dk = dot(ds, qq, 1, 0) * inverse_root
            dv = dot(low, gg, 1, 0)
            dq = (dot(ds, kk, 0, 0) * inverse_root).astype(jnp.bfloat16)
            for n, h in enumerate(heads):
                dq_ref[rows, h] = dq[n * span : (n + 1) * span]
            sent[slot, 0, :, col] = dk[:span].astype(jnp.bfloat16)
            sent[slot, 1, :, col] = dv[:span].astype(jnp.bfloat16)
            own[slot, 0, :, col] = dk[span:]
            own[slot, 1, :, col] = dv[span:]

        @pl.when((me > 0) if slot == 0 else (me < last))
        def _():
            back_copy(slot).start()

    outs = [
        pltpu.make_async_copy(dq_ref, dq_hbm, out_sem.at[0]),
        pltpu.make_async_copy(dv_ref, dv_hbm, out_sem.at[1]),
        pltpu.make_async_copy(dk_ref, dk_hbm, out_sem.at[2]),
        pltpu.make_async_copy(w_ref, w_hbm, out_sem.at[3]),
    ]
    outs[0].start()

    @pl.when(me == last)
    def _():
        back[0] = sent[1]

    for slot in range(2):
        @pl.when((me < last) if slot == 0 else (me > 0))
        def _():
            back_copy(slot).wait_recv()

        rows = pl.ds(slot * span, span)
        dv_ref[rows] = (own[slot, 1] + back[slot, 1].astype(jnp.float32)).astype(jnp.bfloat16)

    def columns(i):
        return pl.ds(pl.multiple_of(i * tokens, tokens), tokens)

    def vg_send(source, target, send_sem, recv_sem):
        return pltpu.make_async_remote_copy(
            src_ref=vg_buf.at[:, columns(source)],
            dst_ref=vg_buf.at[:, columns(source)],
            send_sem=send_sem,
            recv_sem=recv_sem,
            device_id=ctx_id(target),
            device_id_type=MESH,
        )

    vg_buf[:, columns(me)] = dv_ref[...].T
    far = range(n_ctx // 2 - 1)
    for j in far:
        vg_send(me, same_core[j], vg_ss.at[j], vg_rs.at[j]).start()
    pair = vg_send(me, partner, pair_ss, pair_rs)
    pair.start()
    for slot in range(2):
        rows = pl.ds(slot * span, span)
        dk_ref[rows] = (own[slot, 0] + back[slot, 0].astype(jnp.float32)).astype(jnp.bfloat16)
    outs[1].start()
    outs[2].start()
    li_local.wait()
    for j in range(n_ctx - 1):
        li_copy(j).wait_recv()

    def forward(j):
        source = lax.rem(me - 2 * (j + 1) + n_ctx, n_ctx)
        return vg_send(source, partner, fwd_ss.at[j], fwd_rs.at[j])

    for j in far:
        vg_send(me, same_core[j], vg_ss.at[j], vg_rs.at[j]).wait_recv()
        forward(j).start()
    pair.wait_recv()
    for j in far:
        forward(j).wait_recv()

    def lo_copy(c, j):
        peer = lo_peers[j]
        return pltpu.make_async_remote_copy(
            src_ref=part.at[peer, c],
            dst_ref=recv_lo.at[j, c],
            send_sem=lo_ss.at[j, c],
            recv_sem=lo_rs.at[j, c],
            device_id=dp_id(my_hi * n_lo + peer),
            device_id_type=MESH,
        )

    for c in range(pieces):
        product = dot(vg_buf[...], li_buf[:, c * width : (c + 1) * width], 1, 0)
        for h in range(n_hi):
            for l in range(n_lo):
                top = (h * n_lo + l) * blk
                part[l, c, h] = product[top : top + blk].astype(jnp.bfloat16)
        for j in range(n_lo - 1):
            lo_copy(c, j).start()

    def hi_copy(c, j):
        return pltpu.make_async_remote_copy(
            src_ref=part_hi.at[c, hi_peers[j]],
            dst_ref=recv_hi.at[c, j],
            send_sem=hi_ss.at[c, j],
            recv_sem=hi_rs.at[c, j],
            device_id=dp_id(hi_peers[j] * n_lo + my_lo),
            device_id_type=MESH,
        )

    for c in range(pieces):
        for j in range(n_lo - 1):
            lo_copy(c, j).wait_recv()
        total = part[my_lo, c].astype(jnp.float32)
        for j in range(n_lo - 1):
            total = total + recv_lo[j, c].astype(jnp.float32)
        part_hi[c] = total.astype(jnp.bfloat16)
        for j in range(n_hi - 1):
            hi_copy(c, j).start()

    for c in range(pieces):
        total = part[my_lo, c, my_hi].astype(jnp.float32)
        for j in range(n_lo - 1):
            total = total + recv_lo[j, c, my_hi].astype(jnp.float32)
        for j in range(n_hi - 1):
            hi_copy(c, j).wait_recv()
            total = total + recv_hi[c, j].astype(jnp.float32)
        w_ref[:, c * width : (c + 1) * width] = total * (1.0 / (n_hi * n_lo))
    outs[3].start()

    @pl.when(me < last)
    def _():
        for which in range(2):
            halo_copy(0, which).wait_send()
        back_copy(1).wait_send()

    @pl.when(me > 0)
    def _():
        for which in range(2):
            halo_copy(1, which).wait_send()
        back_copy(0).wait_send()

    for j in range(n_ctx - 1):
        li_copy(j).wait_send()
    pair.wait_send()
    for j in far:
        vg_send(me, same_core[j], vg_ss.at[j], vg_rs.at[j]).wait_send()
        forward(j).wait_send()
    for c in range(pieces):
        for j in range(n_lo - 1):
            lo_copy(c, j).wait_send()
        for j in range(n_hi - 1):
            hi_copy(c, j).wait_send()
    for copy in outs:
        copy.wait()


def hand_over(*refs):
    count = len(refs) // 3
    sem = refs[-1]
    fetch = [pltpu.make_async_copy(refs[n], refs[2 * count + n], sem.at[0, n]) for n in range(count)]
    store = [
        pltpu.make_async_copy(refs[2 * count + n], refs[count + n], sem.at[1, n])
        for n in range(count)
    ]
    for copy in fetch:
        copy.start()
    for n in range(count):
        fetch[n].wait()
        store[n].start()
    for copy in store:
        copy.wait()


def body(n_ctx, n_dp, queries, keys, values, out_grad, layer_input, doc_lengths):
    span = queries.shape[3]
    tokens = 2 * span
    q = queries.reshape(tokens, queries.shape[4])
    k = keys.reshape(tokens, keys.shape[4])
    v = values.reshape(tokens, values.shape[4])
    g = out_grad.reshape(tokens, out_grad.shape[4])
    li = layer_input.reshape(tokens, layer_input.shape[4])
    kv_width = k.shape[1]
    kvh = kv_width // HD
    groups = q.shape[1] // kv_width
    chunk = li.shape[1] // n_ctx
    blk = kv_width // n_dp
    n_lo = 2 ** ((n_dp.bit_length() - 1) // 2)
    n_hi = n_dp // n_lo
    width = min(256, chunk)
    pieces = chunk // width
    far = max(1, n_ctx // 2 - 1)
    bf16, f32 = jnp.bfloat16, jnp.float32
    dma = pltpu.SemaphoreType.DMA
    hbm = pl.BlockSpec(memory_space=pltpu.HBM)
    shapes = (
        jax.ShapeDtypeStruct(q.shape, bf16),
        jax.ShapeDtypeStruct(k.shape, bf16),
        jax.ShapeDtypeStruct(v.shape, bf16),
        jax.ShapeDtypeStruct((blk, chunk), f32),
    )
    outs = pl.pallas_call(
        functools.partial(kernel, n_ctx, n_hi, n_lo, span, kvh, groups),
        out_shape=shapes,
        in_specs=[hbm] * 6,
        out_specs=(hbm,) * 4,
        scratch_shapes=[
            pltpu.VMEM(q.shape, bf16),
            pltpu.VMEM(k.shape, bf16),
            pltpu.VMEM(v.shape, bf16),
            pltpu.VMEM((blk, chunk), f32),
            dma((4,)),
            pltpu.VMEM(q.shape, bf16),
            pltpu.VMEM(g.shape, bf16),
            pltpu.SMEM(doc_lengths.shape, jnp.int32),
            pltpu.VMEM((2, 2, 2 * span, kv_width), bf16),
            pltpu.VMEM((2, 2, span, kv_width), bf16),
            pltpu.VMEM((2, 2, span, kv_width), bf16),
            pltpu.VMEM((2, 2, span, kv_width), f32),
            pltpu.VMEM((n_ctx * tokens, chunk), bf16),
            pltpu.VMEM((kv_width, n_ctx * tokens), bf16),
            pltpu.VMEM((n_lo, pieces, n_hi, blk, width), bf16),
            pltpu.VMEM((n_lo - 1, pieces, n_hi, blk, width), bf16),
            pltpu.VMEM((pieces, n_hi, blk, width), bf16),
            pltpu.VMEM((pieces, n_hi - 1, blk, width), bf16),
            dma((3,)), dma((2, 2)), dma((2,)),
            dma((2, 2)), dma((2, 2)), dma((2,)), dma((2,)),
            dma((n_ctx - 1,)), dma((n_ctx - 1,)), dma,
            dma, dma, dma((far,)), dma((far,)), dma((far,)), dma((far,)),
            dma((n_lo - 1, pieces)), dma((n_lo - 1, pieces)),
            dma((pieces, n_hi - 1)), dma((pieces, n_hi - 1)),
        ],
        compiler_params=pltpu.CompilerParams(
            collective_id=0, has_side_effects=True, vmem_limit_bytes=VMEM_LIMIT
        ),
        name="attention_grads",
    )(q, k, v, g, li, doc_lengths)
    dq, dk, dv, w = pl.pallas_call(
        hand_over,
        out_shape=shapes,
        in_specs=[hbm] * 4,
        out_specs=(hbm,) * 4,
        scratch_shapes=[pltpu.VMEM(out.shape, out.dtype) for out in shapes] + [dma((2, 4))],
        compiler_params=pltpu.CompilerParams(vmem_limit_bytes=VMEM_LIMIT),
        name="hand_over",
    )(*outs)
    return (
        dq.reshape(queries.shape),
        dk.reshape(keys.shape),
        dv.reshape(values.shape),
        w.T,
    )


def solution(mesh):
    tokens = P("dp", "ctx", None, None, None)
    return jax.shard_map(
        functools.partial(body, mesh.shape["ctx"], mesh.shape["dp"]),
        mesh=mesh,
        in_specs=(tokens, tokens, tokens, tokens, tokens, P("dp", None)),
        out_specs=(tokens, tokens, tokens, P("ctx", "dp")),
        check_vma=False,
    )
```

```python
import functools
import math

import jax
import jax.numpy as jnp
from jax import lax
from jax.experimental import pallas as pl
from jax.experimental.pallas import tpu as pltpu
from jax.sharding import PartitionSpec as P

HD = 128
MESH = pl.DeviceIdType.MESH
VMEM_LIMIT = 63 * 1024 * 1024


def dot(a, b, ca, cb):
    return lax.dot_general(a, b, (((ca,), (cb,)), ((), ())), preferred_element_type=jnp.float32)


def kernel(
    n_ctx, n_hi, n_lo, span, kvh, groups,
    q_hbm, k_hbm, v_hbm, g_hbm, li_ref, len_hbm,
    dq_hbm, dk_hbm, dv_hbm, w_hbm,
    dq_ref, dk_ref, dv_ref, w_ref, out_sem,
    q_ref, g_ref, len_ref, kv, sent, back, own, li_buf, vg_buf, part, recv_lo, part_hi, recv_hi,
    in_sem, kv_sem, fold_sem, halo_ss, halo_rs, back_ss, back_rs, li_ss, li_rs, li_own,
    pair_ss, pair_rs, vg_ss, vg_rs, fwd_ss, fwd_rs, lo_ss, lo_rs, hi_ss, hi_rs,
):
    me = lax.axis_index("ctx")
    place = lax.axis_index("dp")
    my_hi = place // n_lo
    my_lo = place % n_lo
    last = n_ctx - 1
    tokens = 2 * span
    chunk = li_buf.shape[1]
    pieces, _, blk, width = part.shape[1:]
    inverse_root = 1.0 / math.sqrt(HD)

    def ctx_id(i):
        return (place, i)

    def dp_id(d):
        return (d, me)

    partner = me + 1 - 2 * lax.rem(me, 2)
    same_core = [lax.rem(me + 2 * j, n_ctx) for j in range(1, n_ctx // 2)]
    ctx_peers = [lax.rem(me + j, n_ctx) for j in range(1, n_ctx)]
    lo_peers = [lax.rem(my_lo + j, n_lo) for j in range(1, n_lo)]
    hi_peers = [lax.rem(my_hi + j, n_hi) for j in range(1, n_hi)]

    locals_in = [
        pltpu.make_async_copy(len_hbm, len_ref, in_sem.at[0]),
        pltpu.make_async_copy(q_hbm, q_ref, in_sem.at[1]),
        pltpu.make_async_copy(g_hbm, g_ref, in_sem.at[2]),
    ]
    own_kv = [
        pltpu.make_async_copy(
            source.at[pl.ds(slot * span, span)],
            kv.at[slot, which, pl.ds(span, span)],
            kv_sem.at[slot, which],
        )
        for slot in range(2)
        for which, source in enumerate((k_hbm, v_hbm))
    ]
    fold_kv = [
        pltpu.make_async_copy(
            source.at[pl.ds(0, span)], kv.at[1, which, pl.ds(0, span)], fold_sem.at[which]
        )
        for which, source in enumerate((k_hbm, v_hbm))
    ]
    my_rows = pl.ds(pl.multiple_of(me * tokens, tokens), tokens)
    li_local = pltpu.make_async_copy(
        li_ref.at[:, pl.ds(pl.multiple_of(me * chunk, chunk), chunk)], li_buf.at[my_rows], li_own
    )
    for copy in own_kv + locals_in:
        copy.start()

    barrier = pltpu.get_barrier_semaphore()
    for peer in ctx_peers:
        pl.semaphore_signal(barrier, inc=1, device_id=ctx_id(peer), device_id_type=MESH)
    for peer in lo_peers:
        pl.semaphore_signal(barrier, inc=1, device_id=dp_id(my_hi * n_lo + peer), device_id_type=MESH)
    for peer in hi_peers:
        pl.semaphore_signal(barrier, inc=1, device_id=dp_id(peer * n_lo + my_lo), device_id_type=MESH)

    @pl.when(me == 0)
    def _():
        kv[0, :, pl.ds(0, span)] = jnp.zeros((2, span, kv.shape[3]), kv.dtype)
        for g in range(kvh):
            back[g, 1] = jnp.zeros(back.shape[2:], back.dtype)

    @pl.when(me == last)
    def _():
        for copy in fold_kv:
            copy.start()

    pl.semaphore_wait(barrier, n_ctx + n_lo + n_hi - 3)

    def halo_copy(slot, which):
        source = (k_hbm, v_hbm)[which]
        return pltpu.make_async_remote_copy(
            src_ref=source.at[pl.ds(slot * span, span)],
            dst_ref=kv.at[slot, which, pl.ds(0, span)],
            send_sem=halo_ss.at[slot, which],
            recv_sem=halo_rs.at[slot, which],
            device_id=ctx_id(jnp.minimum(me + 1, last) if slot == 0 else jnp.maximum(me - 1, 0)),
            device_id_type=MESH,
        )

    def back_copy(g, slot):
        return pltpu.make_async_remote_copy(
            src_ref=sent.at[g, slot],
            dst_ref=back.at[g, slot],
            send_sem=back_ss.at[g, slot],
            recv_sem=back_rs.at[g, slot],
            device_id=ctx_id(jnp.maximum(me - 1, 0) if slot == 0 else jnp.minimum(me + 1, last)),
            device_id_type=MESH,
        )

    @pl.when(me < last)
    def _():
        for which in range(2):
            halo_copy(0, which).start()

    @pl.when(me > 0)
    def _():
        for which in range(2):
            halo_copy(1, which).start()

    def li_copy(j):
        peer = ctx_peers[j]
        return pltpu.make_async_remote_copy(
            src_ref=li_ref.at[:, pl.ds(pl.multiple_of(peer * chunk, chunk), chunk)],
            dst_ref=li_buf.at[my_rows],
            send_sem=li_ss.at[j],
            recv_sem=li_rs.at[j],
            device_id=ctx_id(peer),
            device_id_type=MESH,
        )

    for j in range(n_ctx - 1):
        li_copy(j).start()
    li_local.start()
    for copy in own_kv + locals_in:
        copy.wait()

    masks = []
    for slot in range(2):
        stretch = me if slot == 0 else 2 * n_ctx - 1 - me
        first = stretch * span
        lane = lax.broadcasted_iota(jnp.int32, (1, groups * span), 1)
        pos = first + lax.rem(lane, span)
        begin = jnp.zeros_like(pos)
        run = jnp.int32(0)
        for j in range(len_ref.shape[1]):
            begin = jnp.where(pos >= run, run, begin)
            run = run + len_ref[0, j]
        key_pos = first - span + lax.broadcasted_iota(jnp.int32, (2 * span, groups * span), 0)
        masks.append((key_pos >= begin) & (key_pos <= pos))

        @pl.when((me > 0) if slot == 0 else (me < last))
        def _():
            for which in range(2):
                halo_copy(slot, which).wait_recv()

    @pl.when(me == last)
    def _():
        for copy in fold_kv:
            copy.wait()

    def columns(i):
        return pl.ds(pl.multiple_of(i * tokens, tokens), tokens)

    def vg_send(g, source, target, send_sem, recv_sem):
        return pltpu.make_async_remote_copy(
            src_ref=vg_buf.at[pl.ds(g * HD, HD), columns(source)],
            dst_ref=vg_buf.at[pl.ds(g * HD, HD), columns(source)],
            send_sem=send_sem,
            recv_sem=recv_sem,
            device_id=ctx_id(target),
            device_id_type=MESH,
        )

    far = range(n_ctx // 2 - 1)

    def over(g, j):
        return vg_send(g, me, same_core[j], vg_ss.at[g, j], vg_rs.at[g, j])

    def pair(g):
        return vg_send(g, me, partner, pair_ss.at[g], pair_rs.at[g])

    def forward(g, j):
        source = lax.rem(me - 2 * (j + 1) + n_ctx, n_ctx)
        return vg_send(g, source, partner, fwd_ss.at[g, j], fwd_rs.at[g, j])

    def attend(g):
        col = slice(g * HD, (g + 1) * HD)
        heads = [slice(h * HD, (h + 1) * HD) for h in range(g * groups, (g + 1) * groups)]
        for slot in range(2):
            rows = pl.ds(slot * span, span)
            kk = kv[slot, 0, :, col]
            vv = kv[slot, 1, :, col]
            qq = jnp.concatenate([q_ref[rows, h] for h in heads], axis=0)
            gg = jnp.concatenate([g_ref[rows, h] for h in heads], axis=0)
            scores = jnp.where(masks[slot], dot(kk, qq, 1, 1) * inverse_root, -1e30)
            weights = jnp.exp(scores - jnp.max(scores, axis=0, keepdims=True))
            probs = weights * (1.0 / jnp.sum(weights, axis=0, keepdims=True))
            low = probs.astype(jnp.bfloat16)
            dprob = dot(vv, gg, 1, 1)
            delta = jnp.sum(low.astype(jnp.float32) * dprob, axis=0, keepdims=True)
            ds = (probs * (dprob - delta)).astype(jnp.bfloat16)
            dk = dot(ds, qq, 1, 0) * inverse_root
            dv = dot(low, gg, 1, 0)
            dq = (dot(ds, kk, 0, 0) * inverse_root).astype(jnp.bfloat16)
            for n, h in enumerate(heads):
                dq_ref[rows, h] = dq[n * span : (n + 1) * span]
            sent[g, slot, 0] = dk[:span].astype(jnp.bfloat16)
            sent[g, slot, 1] = dv[:span].astype(jnp.bfloat16)
            own[slot, 0, :, col] = dk[span:]
            own[slot, 1, :, col] = dv[span:]

        @pl.when(me > 0)
        def _():
            back_copy(g, 0).start()

        @pl.when(me < last)
        def _():
            back_copy(g, 1).start()

        @pl.when(me == last)
        def _():
            back[g, 0] = sent[g, 1]

    def settle(g):
        @pl.when(me < last)
        def _():
            back_copy(g, 0).wait_recv()

        @pl.when(me > 0)
        def _():
            back_copy(g, 1).wait_recv()

        col = slice(g * HD, (g + 1) * HD)
        for slot in range(2):
            rows = pl.ds(slot * span, span)
            dv_ref[rows, col] = (own[slot, 1, :, col] + back[g, slot, 1].astype(jnp.float32)).astype(
                jnp.bfloat16
            )
        vg_buf[pl.ds(g * HD, HD), columns(me)] = dv_ref[:, col].T
        for j in far:
            over(g, j).start()
        pair(g).start()
        for slot in range(2):
            rows = pl.ds(slot * span, span)
            dk_ref[rows, col] = (own[slot, 0, :, col] + back[g, slot, 0].astype(jnp.float32)).astype(
                jnp.bfloat16
            )

    def pass_on(g):
        for j in far:
            over(g, j).wait_recv()
            forward(g, j).start()

    for g in range(kvh):
        attend(g)
        if g >= 1:
            settle(g - 1)
    settle(kvh - 1)

    outs = [
        pltpu.make_async_copy(dq_ref, dq_hbm, out_sem.at[0]),
        pltpu.make_async_copy(dv_ref, dv_hbm, out_sem.at[1]),
        pltpu.make_async_copy(dk_ref, dk_hbm, out_sem.at[2]),
        pltpu.make_async_copy(w_ref, w_hbm, out_sem.at[3]),
    ]
    outs[0].start()

    outs[1].start()
    outs[2].start()
    for g in range(kvh):
        pass_on(g)
    li_local.wait()
    for j in range(n_ctx - 1):
        li_copy(j).wait_recv()
    for g in range(kvh):
        pair(g).wait_recv()
        for j in far:
            forward(g, j).wait_recv()

    def lo_copy(c, j):
        peer = lo_peers[j]
        return pltpu.make_async_remote_copy(
            src_ref=part.at[peer, c],
            dst_ref=recv_lo.at[j, c],
            send_sem=lo_ss.at[j, c],
            recv_sem=lo_rs.at[j, c],
            device_id=dp_id(my_hi * n_lo + peer),
            device_id_type=MESH,
        )

    for c in range(pieces):
        product = dot(vg_buf[...], li_buf[:, c * width : (c + 1) * width], 1, 0)
        for h in range(n_hi):
            for l in range(n_lo):
                top = (h * n_lo + l) * blk
                part[l, c, h] = product[top : top + blk].astype(jnp.bfloat16)
        for j in range(n_lo - 1):
            lo_copy(c, j).start()

    def hi_copy(c, j):
        return pltpu.make_async_remote_copy(
            src_ref=part_hi.at[c, hi_peers[j]],
            dst_ref=recv_hi.at[c, j],
            send_sem=hi_ss.at[c, j],
            recv_sem=hi_rs.at[c, j],
            device_id=dp_id(hi_peers[j] * n_lo + my_lo),
            device_id_type=MESH,
        )

    for c in range(pieces):
        for j in range(n_lo - 1):
            lo_copy(c, j).wait_recv()
        total = part[my_lo, c].astype(jnp.float32)
        for j in range(n_lo - 1):
            total = total + recv_lo[j, c].astype(jnp.float32)
        part_hi[c] = total.astype(jnp.bfloat16)
        for j in range(n_hi - 1):
            hi_copy(c, j).start()

    for c in range(pieces):
        total = part[my_lo, c, my_hi].astype(jnp.float32)
        for j in range(n_lo - 1):
            total = total + recv_lo[j, c, my_hi].astype(jnp.float32)
        for j in range(n_hi - 1):
            hi_copy(c, j).wait_recv()
            total = total + recv_hi[c, j].astype(jnp.float32)
        w_ref[:, c * width : (c + 1) * width] = total * (1.0 / (n_hi * n_lo))
    outs[3].start()

    @pl.when(me < last)
    def _():
        for which in range(2):
            halo_copy(0, which).wait_send()
        for g in range(kvh):
            back_copy(g, 1).wait_send()

    @pl.when(me > 0)
    def _():
        for which in range(2):
            halo_copy(1, which).wait_send()
        for g in range(kvh):
            back_copy(g, 0).wait_send()

    for j in range(n_ctx - 1):
        li_copy(j).wait_send()
    for g in range(kvh):
        pair(g).wait_send()
        for j in far:
            over(g, j).wait_send()
            forward(g, j).wait_send()
    for c in range(pieces):
        for j in range(n_lo - 1):
            lo_copy(c, j).wait_send()
        for j in range(n_hi - 1):
            hi_copy(c, j).wait_send()
    for copy in outs:
        copy.wait()


def hand_over(*refs):
    count = len(refs) // 3
    sem = refs[-1]
    fetch = [pltpu.make_async_copy(refs[n], refs[2 * count + n], sem.at[0, n]) for n in range(count)]
    store = [
        pltpu.make_async_copy(refs[2 * count + n], refs[count + n], sem.at[1, n])
        for n in range(count)
    ]
    for copy in fetch:
        copy.start()
    for n in range(count):
        fetch[n].wait()
        store[n].start()
    for copy in store:
        copy.wait()


def body(n_ctx, n_dp, queries, keys, values, out_grad, layer_input, doc_lengths):
    span = queries.shape[3]
    tokens = 2 * span
    q = queries.reshape(tokens, queries.shape[4])
    k = keys.reshape(tokens, keys.shape[4])
    v = values.reshape(tokens, values.shape[4])
    g = out_grad.reshape(tokens, out_grad.shape[4])
    li = layer_input.reshape(tokens, layer_input.shape[4])
    kv_width = k.shape[1]
    kvh = kv_width // HD
    groups = q.shape[1] // kv_width
    chunk = li.shape[1] // n_ctx
    blk = kv_width // n_dp
    n_lo = 2 ** ((n_dp.bit_length() - 1) // 2)
    n_hi = n_dp // n_lo
    width = min(256, chunk)
    pieces = chunk // width
    far = max(1, n_ctx // 2 - 1)
    bf16, f32 = jnp.bfloat16, jnp.float32
    dma = pltpu.SemaphoreType.DMA
    hbm = pl.BlockSpec(memory_space=pltpu.HBM)
    shapes = (
        jax.ShapeDtypeStruct(q.shape, bf16),
        jax.ShapeDtypeStruct(k.shape, bf16),
        jax.ShapeDtypeStruct(v.shape, bf16),
        jax.ShapeDtypeStruct((blk, chunk), f32),
    )
    outs = pl.pallas_call(
        functools.partial(kernel, n_ctx, n_hi, n_lo, span, kvh, groups),
        out_shape=shapes,
        in_specs=[hbm] * 6,
        out_specs=(hbm,) * 4,
        scratch_shapes=[
            pltpu.VMEM(q.shape, bf16),
            pltpu.VMEM(k.shape, bf16),
            pltpu.VMEM(v.shape, bf16),
            pltpu.VMEM((blk, chunk), f32),
            dma((4,)),
            pltpu.VMEM(q.shape, bf16),
            pltpu.VMEM(g.shape, bf16),
            pltpu.SMEM(doc_lengths.shape, jnp.int32),
            pltpu.VMEM((2, 2, 2 * span, kv_width), bf16),
            pltpu.VMEM((kvh, 2, 2, span, HD), bf16),
            pltpu.VMEM((kvh, 2, 2, span, HD), bf16),
            pltpu.VMEM((2, 2, span, kv_width), f32),
            pltpu.VMEM((n_ctx * tokens, chunk), bf16),
            pltpu.VMEM((kv_width, n_ctx * tokens), bf16),
            pltpu.VMEM((n_lo, pieces, n_hi, blk, width), bf16),
            pltpu.VMEM((n_lo - 1, pieces, n_hi, blk, width), bf16),
            pltpu.VMEM((pieces, n_hi, blk, width), bf16),
            pltpu.VMEM((pieces, n_hi - 1, blk, width), bf16),
            dma((3,)), dma((2, 2)), dma((2,)),
            dma((2, 2)), dma((2, 2)), dma((kvh, 2)), dma((kvh, 2)),
            dma((n_ctx - 1,)), dma((n_ctx - 1,)), dma,
            dma((kvh,)), dma((kvh,)),
            dma((kvh, far)), dma((kvh, far)), dma((kvh, far)), dma((kvh, far)),
            dma((n_lo - 1, pieces)), dma((n_lo - 1, pieces)),
            dma((pieces, n_hi - 1)), dma((pieces, n_hi - 1)),
        ],
        compiler_params=pltpu.CompilerParams(
            collective_id=0, has_side_effects=True, vmem_limit_bytes=VMEM_LIMIT
        ),
        name="attention_grads",
    )(q, k, v, g, li, doc_lengths)
    dq, dk, dv, w = pl.pallas_call(
        hand_over,
        out_shape=shapes,
        in_specs=[hbm] * 4,
        out_specs=(hbm,) * 4,
        scratch_shapes=[pltpu.VMEM(out.shape, out.dtype) for out in shapes] + [dma((2, 4))],
        compiler_params=pltpu.CompilerParams(vmem_limit_bytes=VMEM_LIMIT),
        name="hand_over",
    )(*outs)
    return (
        dq.reshape(queries.shape),
        dk.reshape(keys.shape),
        dv.reshape(values.shape),
        w.T,
    )


def solution(mesh):
    tokens = P("dp", "ctx", None, None, None)
    return jax.shard_map(
        functools.partial(body, mesh.shape["ctx"], mesh.shape["dp"]),
        mesh=mesh,
        in_specs=(tokens, tokens, tokens, tokens, tokens, P("dp", None)),
        out_specs=(tokens, tokens, tokens, P("ctx", "dp")),
        check_vma=False,
    )
```

```python
import functools
import math

import jax
import jax.numpy as jnp
from jax import lax
from jax.experimental import pallas as pl
from jax.experimental.pallas import tpu as pltpu
from jax.sharding import PartitionSpec as P

HD = 128
MESH = pl.DeviceIdType.MESH
VMEM_LIMIT = 63 * 1024 * 1024


def dot(a, b, ca, cb):
    return lax.dot_general(a, b, (((ca,), (cb,)), ((), ())), preferred_element_type=jnp.float32)


def kernel(
    n_ctx, n_hi, n_lo, span, kvh, groups,
    q_hbm, k_hbm, v_hbm, g_hbm, li_ref, len_hbm,
    dq_hbm, dk_hbm, dv_hbm, w_hbm,
    dq_ref, dk_ref, dv_ref, w_ref, out_sem,
    q_ref, g_ref, len_ref, kv, sent, back, own, li_buf, vg_buf, part, recv_lo, part_hi, recv_hi,
    in_sem, kv_sem, fold_sem, halo_ss, halo_rs, back_ss, back_rs, li_ss, li_rs, li_own,
    pair_ss, pair_rs, vg_ss, vg_rs, fwd_ss, fwd_rs, lo_ss, lo_rs, hi_ss, hi_rs,
):
    me = lax.axis_index("ctx")
    place = lax.axis_index("dp")
    my_hi = place // n_lo
    my_lo = place % n_lo
    last = n_ctx - 1
    tokens = 2 * span
    chunk = li_buf.shape[1]
    pieces, _, blk, width = part.shape[1:]
    inverse_root = 1.0 / math.sqrt(HD)

    def ctx_id(i):
        return (place, i)

    def dp_id(d):
        return (d, me)

    partner = me + 1 - 2 * lax.rem(me, 2)
    same_core = [lax.rem(me + 2 * j, n_ctx) for j in range(1, n_ctx // 2)]
    ctx_peers = [lax.rem(me + j, n_ctx) for j in range(1, n_ctx)]
    lo_peers = [lax.rem(my_lo + j, n_lo) for j in range(1, n_lo)]
    hi_peers = [lax.rem(my_hi + j, n_hi) for j in range(1, n_hi)]

    locals_in = [
        pltpu.make_async_copy(len_hbm, len_ref, in_sem.at[0]),
        pltpu.make_async_copy(q_hbm, q_ref, in_sem.at[1]),
        pltpu.make_async_copy(g_hbm, g_ref, in_sem.at[2]),
    ]
    own_kv = [
        pltpu.make_async_copy(
            source.at[pl.ds(slot * span, span)],
            kv.at[slot, which, pl.ds(span, span)],
            kv_sem.at[slot, which],
        )
        for slot in range(2)
        for which, source in enumerate((k_hbm, v_hbm))
    ]
    fold_kv = [
        pltpu.make_async_copy(
            source.at[pl.ds(0, span)], kv.at[1, which, pl.ds(0, span)], fold_sem.at[which]
        )
        for which, source in enumerate((k_hbm, v_hbm))
    ]
    my_rows = pl.ds(pl.multiple_of(me * tokens, tokens), tokens)
    li_local = pltpu.make_async_copy(
        li_ref.at[:, pl.ds(pl.multiple_of(me * chunk, chunk), chunk)], li_buf.at[my_rows], li_own
    )
    for copy in own_kv + locals_in:
        copy.start()

    barrier = pltpu.get_barrier_semaphore()
    for peer in ctx_peers:
        pl.semaphore_signal(barrier, inc=1, device_id=ctx_id(peer), device_id_type=MESH)
    for peer in lo_peers:
        pl.semaphore_signal(barrier, inc=1, device_id=dp_id(my_hi * n_lo + peer), device_id_type=MESH)
    for peer in hi_peers:
        pl.semaphore_signal(barrier, inc=1, device_id=dp_id(peer * n_lo + my_lo), device_id_type=MESH)

    @pl.when(me == 0)
    def _():
        kv[0, :, pl.ds(0, span)] = jnp.zeros((2, span, kv.shape[3]), kv.dtype)
        for g in range(kvh):
            back[g, 1] = jnp.zeros(back.shape[2:], back.dtype)

    @pl.when(me == last)
    def _():
        for copy in fold_kv:
            copy.start()

    pl.semaphore_wait(barrier, n_ctx + n_lo + n_hi - 3)

    def halo_copy(slot, which):
        source = (k_hbm, v_hbm)[which]
        return pltpu.make_async_remote_copy(
            src_ref=source.at[pl.ds(slot * span, span)],
            dst_ref=kv.at[slot, which, pl.ds(0, span)],
            send_sem=halo_ss.at[slot, which],
            recv_sem=halo_rs.at[slot, which],
            device_id=ctx_id(jnp.minimum(me + 1, last) if slot == 0 else jnp.maximum(me - 1, 0)),
            device_id_type=MESH,
        )

    def back_copy(g, slot):
        return pltpu.make_async_remote_copy(
            src_ref=sent.at[g, slot],
            dst_ref=back.at[g, slot],
            send_sem=back_ss.at[g, slot],
            recv_sem=back_rs.at[g, slot],
            device_id=ctx_id(jnp.maximum(me - 1, 0) if slot == 0 else jnp.minimum(me + 1, last)),
            device_id_type=MESH,
        )

    @pl.when(me < last)
    def _():
        for which in range(2):
            halo_copy(0, which).start()

    @pl.when(me > 0)
    def _():
        for which in range(2):
            halo_copy(1, which).start()

    def li_copy(c, j):
        peer = ctx_peers[j]
        return pltpu.make_async_remote_copy(
            src_ref=li_ref.at[:, pl.ds(pl.multiple_of(peer * chunk + c * width, width), width)],
            dst_ref=li_buf.at[my_rows, pl.ds(c * width, width)],
            send_sem=li_ss.at[c, j],
            recv_sem=li_rs.at[c, j],
            device_id=ctx_id(peer),
            device_id_type=MESH,
        )

    early = max(1, pieces // 2)
    for c in range(early):
        for j in range(n_ctx - 1):
            li_copy(c, j).start()
    li_local.start()
    for copy in own_kv + locals_in:
        copy.wait()

    masks = []
    for slot in range(2):
        stretch = me if slot == 0 else 2 * n_ctx - 1 - me
        first = stretch * span
        lane = lax.broadcasted_iota(jnp.int32, (1, groups * span), 1)
        pos = first + lax.rem(lane, span)
        begin = jnp.zeros_like(pos)
        run = jnp.int32(0)
        for j in range(len_ref.shape[1]):
            begin = jnp.where(pos >= run, run, begin)
            run = run + len_ref[0, j]
        key_pos = first - span + lax.broadcasted_iota(jnp.int32, (2 * span, groups * span), 0)
        masks.append((key_pos >= begin) & (key_pos <= pos))

        @pl.when((me > 0) if slot == 0 else (me < last))
        def _():
            for which in range(2):
                halo_copy(slot, which).wait_recv()

    @pl.when(me == last)
    def _():
        for copy in fold_kv:
            copy.wait()

    def columns(i):
        return pl.ds(pl.multiple_of(i * tokens, tokens), tokens)

    def vg_send(g, source, target, send_sem, recv_sem):
        return pltpu.make_async_remote_copy(
            src_ref=vg_buf.at[pl.ds(g * HD, HD), columns(source)],
            dst_ref=vg_buf.at[pl.ds(g * HD, HD), columns(source)],
            send_sem=send_sem,
            recv_sem=recv_sem,
            device_id=ctx_id(target),
            device_id_type=MESH,
        )

    far = range(n_ctx // 2 - 1)

    def over(g, j):
        return vg_send(g, me, same_core[j], vg_ss.at[g, j], vg_rs.at[g, j])

    def pair(g):
        return vg_send(g, me, partner, pair_ss.at[g], pair_rs.at[g])

    def forward(g, j):
        source = lax.rem(me - 2 * (j + 1) + n_ctx, n_ctx)
        return vg_send(g, source, partner, fwd_ss.at[g, j], fwd_rs.at[g, j])

    def attend(g):
        col = slice(g * HD, (g + 1) * HD)
        heads = [slice(h * HD, (h + 1) * HD) for h in range(g * groups, (g + 1) * groups)]
        for slot in range(2):
            rows = pl.ds(slot * span, span)
            kk = kv[slot, 0, :, col]
            vv = kv[slot, 1, :, col]
            qq = jnp.concatenate([q_ref[rows, h] for h in heads], axis=0)
            gg = jnp.concatenate([g_ref[rows, h] for h in heads], axis=0)
            scores = jnp.where(masks[slot], dot(kk, qq, 1, 1) * inverse_root, -1e30)
            weights = jnp.exp(scores - jnp.max(scores, axis=0, keepdims=True))
            probs = weights * (1.0 / jnp.sum(weights, axis=0, keepdims=True))
            low = probs.astype(jnp.bfloat16)
            dprob = dot(vv, gg, 1, 1)
            delta = jnp.sum(low.astype(jnp.float32) * dprob, axis=0, keepdims=True)
            ds = (probs * (dprob - delta)).astype(jnp.bfloat16)
            dk = dot(ds, qq, 1, 0) * inverse_root
            dv = dot(low, gg, 1, 0)
            dq = (dot(ds, kk, 0, 0) * inverse_root).astype(jnp.bfloat16)
            for n, h in enumerate(heads):
                dq_ref[rows, h] = dq[n * span : (n + 1) * span]
            sent[g, slot, 0] = dk[:span].astype(jnp.bfloat16)
            sent[g, slot, 1] = dv[:span].astype(jnp.bfloat16)
            own[slot, 0, :, col] = dk[span:]
            own[slot, 1, :, col] = dv[span:]

        @pl.when(me > 0)
        def _():
            back_copy(g, 0).start()

        @pl.when(me < last)
        def _():
            back_copy(g, 1).start()

        @pl.when(me == last)
        def _():
            back[g, 0] = sent[g, 1]

    def settle(g):
        @pl.when(me < last)
        def _():
            back_copy(g, 0).wait_recv()

        @pl.when(me > 0)
        def _():
            back_copy(g, 1).wait_recv()

        col = slice(g * HD, (g + 1) * HD)
        for slot in range(2):
            rows = pl.ds(slot * span, span)
            dv_ref[rows, col] = (own[slot, 1, :, col] + back[g, slot, 1].astype(jnp.float32)).astype(
                jnp.bfloat16
            )
        vg_buf[pl.ds(g * HD, HD), columns(me)] = dv_ref[:, col].T
        for j in far:
            over(g, j).start()
        pair(g).start()
        for slot in range(2):
            rows = pl.ds(slot * span, span)
            dk_ref[rows, col] = (own[slot, 0, :, col] + back[g, slot, 0].astype(jnp.float32)).astype(
                jnp.bfloat16
            )

    def pass_on(g):
        for j in far:
            over(g, j).wait_recv()
            forward(g, j).start()

    for g in range(kvh):
        attend(g)
        if g >= 1:
            settle(g - 1)
    settle(kvh - 1)
    for c in range(early, pieces):
        for j in range(n_ctx - 1):
            li_copy(c, j).start()

    outs = [
        pltpu.make_async_copy(dq_ref, dq_hbm, out_sem.at[0]),
        pltpu.make_async_copy(dv_ref, dv_hbm, out_sem.at[1]),
        pltpu.make_async_copy(dk_ref, dk_hbm, out_sem.at[2]),
        pltpu.make_async_copy(w_ref, w_hbm, out_sem.at[3]),
    ]
    outs[0].start()

    outs[1].start()
    outs[2].start()
    for g in range(kvh):
        pass_on(g)
    li_local.wait()
    for g in range(kvh):
        pair(g).wait_recv()
        for j in far:
            forward(g, j).wait_recv()

    def lo_copy(c, j):
        peer = lo_peers[j]
        return pltpu.make_async_remote_copy(
            src_ref=part.at[peer, c],
            dst_ref=recv_lo.at[j, c],
            send_sem=lo_ss.at[j, c],
            recv_sem=lo_rs.at[j, c],
            device_id=dp_id(my_hi * n_lo + peer),
            device_id_type=MESH,
        )

    def hi_copy(c, j):
        return pltpu.make_async_remote_copy(
            src_ref=part_hi.at[c, hi_peers[j]],
            dst_ref=recv_hi.at[c, j],
            send_sem=hi_ss.at[c, j],
            recv_sem=hi_rs.at[c, j],
            device_id=dp_id(hi_peers[j] * n_lo + my_lo),
            device_id_type=MESH,
        )

    def multiply(c):
        for j in range(n_ctx - 1):
            li_copy(c, j).wait_recv()
        product = dot(vg_buf[...], li_buf[:, c * width : (c + 1) * width], 1, 0)
        for h in range(n_hi):
            for l in range(n_lo):
                top = (h * n_lo + l) * blk
                part[l, c, h] = product[top : top + blk].astype(jnp.bfloat16)
        for j in range(n_lo - 1):
            lo_copy(c, j).start()

    def reduce(c):
        for j in range(n_lo - 1):
            lo_copy(c, j).wait_recv()
        total = part[my_lo, c].astype(jnp.float32)
        for j in range(n_lo - 1):
            total = total + recv_lo[j, c].astype(jnp.float32)
        part_hi[c] = total.astype(jnp.bfloat16)
        for j in range(n_hi - 1):
            hi_copy(c, j).start()

    for c in range(pieces):
        multiply(c)
        if c >= 1:
            reduce(c - 1)
    reduce(pieces - 1)

    for c in range(pieces):
        total = part[my_lo, c, my_hi].astype(jnp.float32)
        for j in range(n_lo - 1):
            total = total + recv_lo[j, c, my_hi].astype(jnp.float32)
        for j in range(n_hi - 1):
            hi_copy(c, j).wait_recv()
            total = total + recv_hi[c, j].astype(jnp.float32)
        w_ref[:, c * width : (c + 1) * width] = total * (1.0 / (n_hi * n_lo))
    outs[3].start()

    @pl.when(me < last)
    def _():
        for which in range(2):
            halo_copy(0, which).wait_send()
        for g in range(kvh):
            back_copy(g, 1).wait_send()

    @pl.when(me > 0)
    def _():
        for which in range(2):
            halo_copy(1, which).wait_send()
        for g in range(kvh):
            back_copy(g, 0).wait_send()

    for c in range(pieces):
        for j in range(n_ctx - 1):
            li_copy(c, j).wait_send()
    for g in range(kvh):
        pair(g).wait_send()
        for j in far:
            over(g, j).wait_send()
            forward(g, j).wait_send()
    for c in range(pieces):
        for j in range(n_lo - 1):
            lo_copy(c, j).wait_send()
        for j in range(n_hi - 1):
            hi_copy(c, j).wait_send()
    for copy in outs:
        copy.wait()


def hand_over(*refs):
    count = len(refs) // 3
    sem = refs[-1]
    fetch = [pltpu.make_async_copy(refs[n], refs[2 * count + n], sem.at[0, n]) for n in range(count)]
    store = [
        pltpu.make_async_copy(refs[2 * count + n], refs[count + n], sem.at[1, n])
        for n in range(count)
    ]
    for copy in fetch:
        copy.start()
    for n in range(count):
        fetch[n].wait()
        store[n].start()
    for copy in store:
        copy.wait()


def body(n_ctx, n_dp, queries, keys, values, out_grad, layer_input, doc_lengths):
    span = queries.shape[3]
    tokens = 2 * span
    q = queries.reshape(tokens, queries.shape[4])
    k = keys.reshape(tokens, keys.shape[4])
    v = values.reshape(tokens, values.shape[4])
    g = out_grad.reshape(tokens, out_grad.shape[4])
    li = layer_input.reshape(tokens, layer_input.shape[4])
    kv_width = k.shape[1]
    kvh = kv_width // HD
    groups = q.shape[1] // kv_width
    chunk = li.shape[1] // n_ctx
    blk = kv_width // n_dp
    n_lo = 2 ** ((n_dp.bit_length() - 1) // 2)
    n_hi = n_dp // n_lo
    width = min(256, chunk)
    pieces = chunk // width
    far = max(1, n_ctx // 2 - 1)
    bf16, f32 = jnp.bfloat16, jnp.float32
    dma = pltpu.SemaphoreType.DMA
    hbm = pl.BlockSpec(memory_space=pltpu.HBM)
    shapes = (
        jax.ShapeDtypeStruct(q.shape, bf16),
        jax.ShapeDtypeStruct(k.shape, bf16),
        jax.ShapeDtypeStruct(v.shape, bf16),
        jax.ShapeDtypeStruct((blk, chunk), f32),
    )
    outs = pl.pallas_call(
        functools.partial(kernel, n_ctx, n_hi, n_lo, span, kvh, groups),
        out_shape=shapes,
        in_specs=[hbm] * 6,
        out_specs=(hbm,) * 4,
        scratch_shapes=[
            pltpu.VMEM(q.shape, bf16),
            pltpu.VMEM(k.shape, bf16),
            pltpu.VMEM(v.shape, bf16),
            pltpu.VMEM((blk, chunk), f32),
            dma((4,)),
            pltpu.VMEM(q.shape, bf16),
            pltpu.VMEM(g.shape, bf16),
            pltpu.SMEM(doc_lengths.shape, jnp.int32),
            pltpu.VMEM((2, 2, 2 * span, kv_width), bf16),
            pltpu.VMEM((kvh, 2, 2, span, HD), bf16),
            pltpu.VMEM((kvh, 2, 2, span, HD), bf16),
            pltpu.VMEM((2, 2, span, kv_width), f32),
            pltpu.VMEM((n_ctx * tokens, chunk), bf16),
            pltpu.VMEM((kv_width, n_ctx * tokens), bf16),
            pltpu.VMEM((n_lo, pieces, n_hi, blk, width), bf16),
            pltpu.VMEM((n_lo - 1, pieces, n_hi, blk, width), bf16),
            pltpu.VMEM((pieces, n_hi, blk, width), bf16),
            pltpu.VMEM((pieces, n_hi - 1, blk, width), bf16),
            dma((3,)), dma((2, 2)), dma((2,)),
            dma((2, 2)), dma((2, 2)), dma((kvh, 2)), dma((kvh, 2)),
            dma((pieces, n_ctx - 1)), dma((pieces, n_ctx - 1)), dma,
            dma((kvh,)), dma((kvh,)),
            dma((kvh, far)), dma((kvh, far)), dma((kvh, far)), dma((kvh, far)),
            dma((n_lo - 1, pieces)), dma((n_lo - 1, pieces)),
            dma((pieces, n_hi - 1)), dma((pieces, n_hi - 1)),
        ],
        compiler_params=pltpu.CompilerParams(
            collective_id=0, has_side_effects=True, vmem_limit_bytes=VMEM_LIMIT
        ),
        name="attention_grads",
    )(q, k, v, g, li, doc_lengths)
    dq, dk, dv, w = pl.pallas_call(
        hand_over,
        out_shape=shapes,
        in_specs=[hbm] * 4,
        out_specs=(hbm,) * 4,
        scratch_shapes=[pltpu.VMEM(out.shape, out.dtype) for out in shapes] + [dma((2, 4))],
        compiler_params=pltpu.CompilerParams(vmem_limit_bytes=VMEM_LIMIT),
        name="hand_over",
    )(*outs)
    return (
        dq.reshape(queries.shape),
        dk.reshape(keys.shape),
        dv.reshape(values.shape),
        w.T,
    )


def solution(mesh):
    tokens = P("dp", "ctx", None, None, None)
    return jax.shard_map(
        functools.partial(body, mesh.shape["ctx"], mesh.shape["dp"]),
        mesh=mesh,
        in_specs=(tokens, tokens, tokens, tokens, tokens, P("dp", None)),
        out_specs=(tokens, tokens, tokens, P("ctx", "dp")),
        check_vma=False,
    )
```
